128 devices in a mesh: rows: 16 (over z, x), table: 8 (over y, core).
Axes of the slice: x: 4, y: 4, z: 4, core: 2. Of those that a mesh axis runs over, the one named last changes fastest.
Arguments:
- item_table: bfloat16 [2097152, 128], P(('rows', 'table')), may hold values from -40 to 40, as said below
- user_rows: float32 [8192, 128], P(('rows', 'table')), may hold values from -3 to 3
- link_rows: int32 [8192, 128], P(('rows', 'table')), may hold values from 0 to 16383
- link_slots: int32 [8192, 128], P(('rows', 'table')), may hold values from 0 to 8191, as said below
- link_weights: int32 [8192, 128], P(('rows', 'table')), may hold values from 1 to 63
- link_counts: int32 [8192], P(('rows', 'table')), may hold values from 1 to 128
Outputs:
- solved_rows: float32 [8192, 128], P(('rows', 'table'))
The draws below stay inside these ranges and needn't reach their ends.
Inputs may be any that keep to these rules, and one draw needn't show every extreme that they name: `item_table`: rows differ in scale; values lie within the stated bounds. `link_slots`: on each device (flat index over rows then table, users in blocks of 64), its 8192 entries hold every number of 0 to 8191 exactly once; entry s names slot s % 64 toward the device of flat index s // 64, which holds the linked item, so every device names exactly 64 slots of every owner, live or not.
All inputs are finite; a program needn't handle non-finite values.
Results may differ from the reference program's by a relative error of at most 0.0019.
Values may be sent and summed in bfloat16 or wider, within the bound.
No kernel may reach another device: no remote copies, remote signals or barrier semaphores. Data moves between devices by JAX's collectives and lax.ppermute only.
A program may use at most 64 MiB of HBM per device.

```python
import math
import jax
import jax.numpy as jnp
import numpy as np
from jax import lax

K = 128
L = 128
CG_STEPS = 3
U_DEV = 64
ITEM_DEV = 16384
USERS = 8192
ITEMS = 2097152
CAP = 64
N_ROWS = 16
N_TABLE = 8


def draw_item_table(key, part):
    key = jax.random.fold_in(key, 11)
    key_noise, key_scale, key_center = jax.random.split(key, 3)
    ramp = (jnp.arange(ITEMS) // ITEM_DEV).astype(jnp.float32) / max(ITEMS // ITEM_DEV - 1, 1)
    noise = jnp.clip(jax.random.normal(key_noise, (ITEMS, K), jnp.float32), -4.0, 4.0)
    row_scale = 0.3 * jnp.exp(jax.random.uniform(key_scale, (ITEMS, 1), jnp.float32) * jnp.log(10.0))
    center = jax.random.uniform(key_center, (1, K), jnp.float32, -1.0, 1.0)
    ramp_scale = jnp.exp(ramp * 0.5 * jnp.log(3.0))
    return ((noise + center) * row_scale * ramp_scale[:, None]).astype(jnp.bfloat16)


def draw_link_slots(key, part):
    key = jax.random.fold_in(key, 23)
    device_keys = jax.random.split(key, ITEMS // ITEM_DEV)
    orders = jax.vmap(lambda single: jax.random.permutation(single, U_DEV * L))(device_keys)
    return orders.reshape(USERS, L).astype(jnp.int32)


def place_ends(result, stream_key, least, top_value):
    place = [jax.random.randint(jax.random.fold_in(stream_key, axis), (), 0, length) for axis, length in enumerate(result.shape)]
    main_axis = result.shape.index(max(result.shape))
    neighbour = place[:main_axis] + [(place[main_axis] + 1) % result.shape[main_axis]] + place[main_axis + 1:]
    return result.at[tuple(place)].set(least).at[tuple(neighbour)].set(top_value)


def block_levels(rng, extent, cuts, smallest, largest):
    gain, own = 1.0, jax.random.fold_in(rng, 6)
    for axis_at, parts in cuts:
        draws = jnp.exp(jax.random.uniform(jax.random.fold_in(own, axis_at), (parts,), jnp.float32, smallest / len(cuts), largest / len(cuts)))
        gain = gain * jnp.repeat(draws, extent[axis_at] // parts).reshape([-1 if axis == axis_at else 1 for axis in range(len(extent))])
    return gain


def cumulative_ranks(amount, slope):
    weights = [(1 << 20) // math.isqrt(rank ** slope) + 1 for rank in range(1, amount + 1)]
    spread = 1 + sum(weights) // (1 << 30)
    return np.cumsum(np.array([max(1, weight // spread) for weight in weights]))


def ranked_ids(key, shape, count, slope):
    table = cumulative_ranks(count, slope)
    lot = jax.random.randint(jax.random.fold_in(key, 1), shape, 0, int(table[count - 1]))
    rank = jnp.searchsorted(jnp.asarray(table, jnp.int32), lot, side="right")
    return jax.random.permutation(jax.random.fold_in(key, 2), count)[rank].astype(jnp.int32)


def gaussian(key, shape, width, reach, cuts=(), kind=jnp.bfloat16):
    entries = width * jax.random.normal(key, shape, jnp.float32)
    if cuts:
        entries = entries * block_levels(key, shape, cuts, -0.22, 0.18)
    return jnp.clip(entries, -reach, reach).astype(kind)


def setup_inputs(seed: int = 0) -> dict:
    keys = jax.random.split(jax.random.key(seed), 7)
    item_table = draw_item_table(jax.random.fold_in(keys[6], 71), 0)
    user_rows = gaussian(keys[1], (USERS, K), 0.5, 3.0, ((0, 128),), jnp.float32)
    link_rows = place_ends(ranked_ids(keys[2], (USERS, L), ITEM_DEV, 2), jax.random.fold_in(keys[2], 3), 0, ITEM_DEV - 1).astype(jnp.int32)
    link_slots = draw_link_slots(jax.random.fold_in(keys[6], 71), 0)
    link_weights = place_ends(jax.random.randint(keys[4], (USERS, L), 1, 64), jax.random.fold_in(keys[4], 1), 1, 63).astype(jnp.int32)
    link_counts = place_ends(jax.random.randint(keys[5], (USERS,), 1, L + 1), jax.random.fold_in(keys[5], 1), 1, L).astype(jnp.int32)
    return {"item_table": item_table, "user_rows": user_rows, "link_rows": link_rows, "link_slots": link_slots, "link_weights": link_weights, "link_counts": link_counts}


def refine(apply_system, target, initial):
    estimate = initial
    residual = target - apply_system(estimate)
    direction = residual
    norm_now = jnp.sum(residual * residual, axis=1, keepdims=True)
    for iteration in range(CG_STEPS):
        image = apply_system(direction)
        curvature = jnp.sum(direction * image, axis=1, keepdims=True)
        step_len = norm_now / (curvature + 1e-6)
        estimate = estimate + step_len * direction
        residual = residual - step_len * image
        norm_next = jnp.sum(residual * residual, axis=1, keepdims=True)
        direction = residual + (norm_next / (norm_now + 1e-6)) * direction
        norm_now = norm_next
    return estimate


def reference(item_table, user_rows, link_rows, link_slots, link_weights, link_counts):
    device_count = N_ROWS * N_TABLE
    gramian = jnp.dot(item_table.T, item_table, preferred_element_type=jnp.float32)
    shared = gramian * (L / ITEMS) + (0.5 * L) * jnp.eye(K, dtype=jnp.float32)
    owners = (link_slots // CAP).astype(jnp.int32)
    item_ids = (owners * ITEM_DEV + link_rows).astype(jnp.int32)

    def solve_block(pieces):
        ids_block, weight_block, count_block, start_block = pieces
        fetched = item_table[ids_block]
        live_mask = jnp.arange(L, dtype=jnp.int32)[None, :] < count_block[:, None]
        confidence = jnp.where(live_mask, 1.0 + weight_block.astype(jnp.float32) / 8.0, 0.0).astype(jnp.float32)
        scaled = (confidence[:, :, None] * fetched.astype(jnp.float32)).astype(jnp.bfloat16)
        weighted = jnp.einsum("ulk,ulm->ukm", scaled.astype(jnp.float32), fetched.astype(jnp.float32), precision=lax.Precision.HIGHEST)
        system = shared[None, :, :] + weighted
        target = jnp.sum(scaled.astype(jnp.float32), axis=1)

        def apply_system(vector):
            return jnp.einsum("ukm,um->uk", system, vector, precision=lax.Precision.HIGHEST)

        return refine(apply_system, target, start_block)

    solved = lax.map(solve_block, (item_ids.reshape(device_count, U_DEV, L), link_weights.reshape(device_count, U_DEV, L), link_counts.reshape(device_count, U_DEV), user_rows.reshape(device_count, U_DEV, K)))
    return solved.reshape(USERS, K)
```

```python
import functools

import jax
import jax.numpy as jnp
from jax import lax
from jax.experimental import pallas as pl
from jax.experimental.pallas import tpu as pltpu
from jax.sharding import PartitionSpec as P

CG_STEPS = 3
AXES = ("rows", "table")
VMEM_LIMIT = 48 * 2**20
NT = (((1,), (1,)), ((), ()))


def place_kernel(slots_ref, rows_ref, out_ref):
    users, links = slots_ref.shape
    devices, capacity = out_ref.shape
    owner_id = lax.broadcasted_iota(jnp.int32, (devices, links), 0)
    lane_id = lax.broadcasted_iota(jnp.int32, (2 * capacity, links), 0)
    upper = lane_id < capacity
    slot_id = jnp.where(upper, lane_id, lane_id - capacity)
    total = jnp.zeros((devices, 2 * capacity), jnp.float32)
    for user in range(0, users, 2):
        owners, named = [], []
        for one in (user, user + 1):
            slots = slots_ref[one : one + 1, :]
            rows = rows_ref[one : one + 1, :]
            owner = slots // capacity
            place = slots - owner * capacity
            high = (rows // 128).astype(jnp.float32)
            low = (rows % 128).astype(jnp.float32)
            owners.append(jnp.where(owner_id == owner, 1.0, 0.0).astype(jnp.bfloat16))
            value = jnp.where(upper, high, low)
            named.append(jnp.where(slot_id == place, value, 0.0).astype(jnp.bfloat16))
        total = total + lax.dot_general(
            jnp.concatenate(owners, axis=1),
            jnp.concatenate(named, axis=1),
            NT,
            preferred_element_type=jnp.float32,
        )
    high, low = total[:, :capacity], total[:, capacity:]
    out_ref[...] = (high * 128.0 + low).astype(jnp.int32)


def place_requests(link_slots, link_rows, devices, capacity):
    return pl.pallas_call(
        place_kernel,
        out_shape=jax.ShapeDtypeStruct((devices, capacity), jnp.int32),
        in_specs=[pl.BlockSpec(memory_space=pltpu.VMEM)] * 2,
        out_specs=pl.BlockSpec(memory_space=pltpu.VMEM),
        compiler_params=pltpu.CompilerParams(vmem_limit_bytes=VMEM_LIMIT),
        cost_estimate=pl.CostEstimate(flops=2 * 8192 * 128 * 128, bytes_accessed=98304, transcendentals=0),
    )(link_slots, link_rows)


def widen(source_ref, wide_ref, step):
    def one(block, carry):
        start = pl.multiple_of(block * step, step)
        wide_ref[pl.ds(start, step), :] = source_ref[pl.ds(start, step), :].astype(jnp.float32)
        return carry

    lax.fori_loop(0, source_ref.shape[0] // step, one, 0)


def fetch_kernel(index_ref, table_ref, out_ref, wide_ref):
    devices, capacity = index_ref.shape
    widen(table_ref, wide_ref, 256)

    def one(device, carry):
        rows = [wide_ref[pl.ds(index_ref[device, slot], 1), :] for slot in range(capacity)]
        out_ref[device] = jnp.concatenate(rows, axis=0).astype(jnp.bfloat16)
        return carry

    lax.fori_loop(0, devices, one, 0)


def fetch_rows(asked, item_table):
    devices, capacity = asked.shape
    items, features = item_table.shape
    return pl.pallas_call(
        fetch_kernel,
        out_shape=jax.ShapeDtypeStruct((devices, capacity, features), jnp.bfloat16),
        in_specs=[pl.BlockSpec(memory_space=pltpu.SMEM), pl.BlockSpec(memory_space=pltpu.VMEM)],
        out_specs=pl.BlockSpec(memory_space=pltpu.VMEM),
        scratch_shapes=[pltpu.VMEM((items, features), jnp.float32)],
        compiler_params=pltpu.CompilerParams(vmem_limit_bytes=VMEM_LIMIT),
        cost_estimate=pl.CostEstimate(flops=0, bytes_accessed=24 * 2**20, transcendentals=0),
    )(asked, item_table)


def split(value):
    high = value.astype(jnp.bfloat16)
    low = (value - high.astype(jnp.float32)).astype(jnp.bfloat16)
    return high, low


def solve_kernel(
    slots_ref, arrived_ref, weights_ref, counts_ref, start_ref, shared_ref, out_ref, wide_ref, conf_ref, system_ref
):
    users, links = slots_ref.shape
    features = arrived_ref.shape[1]
    widen(arrived_ref, wide_ref, 256)
    link_id = lax.broadcasted_iota(jnp.int32, (users, links), 1)
    conf_ref[...] = jnp.where(
        link_id < counts_ref[...], 1.0 + weights_ref[...].astype(jnp.float32) / 8.0, 0.0
    )
    user_lane = lax.broadcasted_iota(jnp.int32, (features, 2 * users), 1)
    user_lane = jnp.where(user_lane < users, user_lane, user_lane - users)
    ones = jnp.ones((links, features), jnp.bfloat16)

    def form(user, target):
        rows = [wide_ref[pl.ds(slots_ref[user, link], 1), :] for link in range(links)]
        fetched = jnp.concatenate(rows, axis=0)
        scaled = (fetched.T * conf_ref[pl.ds(user, 1), :]).astype(jnp.bfloat16)
        both = jnp.dot(
            scaled,
            jnp.concatenate([fetched.astype(jnp.bfloat16), ones], axis=1),
            preferred_element_type=jnp.float32,
        )
        high, low = split(both[:, :features])
        start = pl.multiple_of(user * features, features)
        system_ref[pl.ds(start, features), :features] = high
        system_ref[pl.ds(start, features), features:] = low
        return jnp.where(user_lane == user, both[:, features:], target)

    target = lax.fori_loop(0, users, form, jnp.zeros((features, 2 * users), jnp.float32))
    shared = jnp.concatenate(split(shared_ref[...]), axis=1)
    first_half = lax.broadcasted_iota(jnp.int32, (features, 2 * users), 1) < users
    together = 4

    def apply_system(vector):
        high, low = split(vector)
        half = jnp.where(first_half, high.astype(jnp.float32), low.astype(jnp.float32)).astype(jnp.bfloat16)
        operand = jnp.concatenate([half, half], axis=0)

        def some(block, image):
            start = pl.multiple_of(block * together * features, together * features)
            product = jnp.dot(
                system_ref[pl.ds(start, together * features), :], operand, preferred_element_type=jnp.float32
            )
            for one in range(together):
                piece = product[one * features : (one + 1) * features]
                image = jnp.where(user_lane == block * together + one, piece, image)
            return image

        image = lax.fori_loop(0, users // together, some, jnp.zeros((features, 2 * users), jnp.float32))
        image = image + jnp.dot(shared, operand, preferred_element_type=jnp.float32)
        return image + pltpu.roll(image, users, 1)

    start_rows = start_ref[...]
    estimate = jnp.concatenate([start_rows, start_rows], axis=0).T
    residual = target - apply_system(estimate)
    direction = residual
    norm_now = jnp.sum(residual * residual, axis=0, keepdims=True)
    for _ in range(CG_STEPS):
        image = apply_system(direction)
        curvature = jnp.sum(direction * image, axis=0, keepdims=True)
        step_len = norm_now / (curvature + 1e-06)
        estimate = estimate + step_len * direction
        residual = residual - step_len * image
        norm_next = jnp.sum(residual * residual, axis=0, keepdims=True)
        direction = residual + norm_next / (norm_now + 1e-06) * direction
        norm_now = norm_next
    out_ref[...] = estimate.T[:users]


def solve_rows(link_slots, arrived, link_weights, link_counts, user_rows, shared):
    users, links = link_slots.shape
    features = user_rows.shape[1]
    vmem = pl.BlockSpec(memory_space=pltpu.VMEM)
    return pl.pallas_call(
        solve_kernel,
        out_shape=jax.ShapeDtypeStruct((users, features), jnp.float32),
        in_specs=[pl.BlockSpec(memory_space=pltpu.SMEM)] + [vmem] * 5,
        out_specs=vmem,
        scratch_shapes=[
            pltpu.VMEM(arrived.shape, jnp.float32),
            pltpu.VMEM((users, links), jnp.float32),
            pltpu.VMEM((users * features, 2 * features), jnp.bfloat16),
        ],
        compiler_params=pltpu.CompilerParams(vmem_limit_bytes=VMEM_LIMIT),
        cost_estimate=pl.CostEstimate(flops=2**32, bytes_accessed=24 * 2**20, transcendentals=0),
    )(link_slots, arrived, link_weights, link_counts.reshape(users, 1), user_rows, shared)


def exchange(value):
    return lax.all_to_all(value, AXES, split_axis=0, concat_axis=0, tiled=True)


def per_device(item_table, user_rows, link_rows, link_slots, link_weights, link_counts):
    users, features = user_rows.shape
    links = link_rows.shape[1]
    devices = lax.axis_size("rows") * lax.axis_size("table")
    capacity = users * links // devices
    total_items = item_table.shape[0] * devices
    asked = exchange(place_requests(link_slots, link_rows, devices, capacity))
    arrived = exchange(fetch_rows(asked, item_table)).reshape(users * links, features)
    partial = jnp.dot(item_table.T, item_table, preferred_element_type=jnp.float32)
    own_row = jnp.sum(exchange(partial), axis=0, keepdims=True)
    gramian = exchange(jnp.broadcast_to(own_row, (features, features)))
    shared = gramian * (links / total_items) + 0.5 * links * jnp.eye(features, dtype=jnp.float32)
    return solve_rows(link_slots, arrived, link_weights, link_counts, user_rows, shared)


def solution(mesh):
    placed = (P(AXES, None),) * 5 + (P(AXES),)
    return jax.shard_map(
        per_device,
        mesh=mesh,
        in_specs=placed,
        out_specs=P(AXES, None),
        check_vma=False,
    )
```

```python
import functools

import jax
import jax.numpy as jnp
from jax import lax
from jax.experimental import pallas as pl
from jax.experimental.pallas import tpu as pltpu
from jax.sharding import PartitionSpec as P

CG_STEPS = 3
BATCH = 32
TOGETHER = 8
AXES = ("rows", "table")
VMEM_LIMIT = 60 * 2**20
NT = (((1,), (1,)), ((), ()))
TN = (((0,), (0,)), ((), ()))
TABLE_STEP = 2048
FETCH_UNROLL = 4
TAIL = 8


def ask_kernel(slots_hbm, rows_hbm, table_hbm, out_ref, slots_ref, rows_ref, table_ref, sems):
    copies = [
        pltpu.make_async_copy(source, target, sems.at[at])
        for at, (source, target) in enumerate(
            ((slots_hbm, slots_ref), (rows_hbm, rows_ref), (table_hbm, table_ref))
        )
    ]
    for copy in copies:
        copy.start()
    users, links = slots_ref.shape
    devices = out_ref.shape[0]
    items, features = table_ref.shape
    capacity = users * links // devices
    owner_id = lax.broadcasted_iota(jnp.int32, (devices, links), 0)
    lane_id = lax.broadcasted_iota(jnp.int32, (2 * capacity, links), 0)
    upper = lane_id < capacity
    slot_id = jnp.where(upper, lane_id, lane_id - capacity)
    copies[0].wait()
    copies[1].wait()
    total = jnp.zeros((devices, 2 * capacity), jnp.float32)
    for user in range(0, users, 2):
        owners, named = [], []
        for one in (user, user + 1):
            slots = slots_ref[one : one + 1, :]
            rows = rows_ref[one : one + 1, :]
            owner = slots // capacity
            place = slots - owner * capacity
            high = (rows // 128).astype(jnp.float32)
            low = (rows % 128).astype(jnp.float32)
            owners.append(jnp.where(owner_id == owner, 1.0, 0.0).astype(jnp.bfloat16))
            value = jnp.where(upper, high, low)
            named.append(jnp.where(slot_id == place, value, 0.0).astype(jnp.bfloat16))
        total = total + lax.dot_general(
            jnp.concatenate(owners, axis=1),
            jnp.concatenate(named, axis=1),
            NT,
            preferred_element_type=jnp.float32,
        )
    asked = total * 128.0 + pltpu.roll(total, capacity, 1)
    lane = lax.broadcasted_iota(jnp.int32, asked.shape, 1)
    out_ref[:, : 2 * capacity] = jnp.where(lane < capacity, asked, 0.0)
    copies[2].wait()
    gramian = jnp.zeros((features, features), jnp.float32)
    for start in range(0, items, TABLE_STEP):
        block = table_ref[start : start + TABLE_STEP, :]
        gramian = gramian + lax.dot_general(block, block, TN, preferred_element_type=jnp.float32)
    out_ref[:, 2 * capacity :] = gramian


def ask(link_slots, link_rows, item_table, devices):
    users, links = link_slots.shape
    features = item_table.shape[1]
    capacity = users * links // devices
    return pl.pallas_call(
        ask_kernel,
        out_shape=jax.ShapeDtypeStruct((devices, 2 * capacity + features), jnp.float32),
        in_specs=[pl.BlockSpec(memory_space=pl.ANY)] * 3,
        out_specs=pl.BlockSpec(memory_space=pltpu.VMEM),
        scratch_shapes=[
            pltpu.VMEM(link_slots.shape, jnp.int32),
            pltpu.VMEM(link_rows.shape, jnp.int32),
            pltpu.VMEM(item_table.shape, jnp.bfloat16),
            pltpu.SemaphoreType.DMA((3,)),
        ],
        compiler_params=pltpu.CompilerParams(vmem_limit_bytes=VMEM_LIMIT),
        cost_estimate=pl.CostEstimate(flops=2**30, bytes_accessed=2**22, transcendentals=0),
    )(link_slots, link_rows, item_table)


def fetch_kernel(received_ref, table_hbm, out_ref, table_ref, wide_ref, index_vmem, index_ref, table_sems, index_sem):
    items, features = table_ref.shape
    devices, held, _ = out_ref.shape
    capacity = held - TAIL
    parts = items // TABLE_STEP
    copies = []
    for part in range(parts):
        span = pl.ds(part * TABLE_STEP, TABLE_STEP)
        copies.append(pltpu.make_async_copy(table_hbm.at[span], table_ref.at[span], table_sems.at[part]))
        copies[-1].start()
    index_vmem[...] = received_ref[:, : 2 * capacity].astype(jnp.int32)
    index_copy = pltpu.make_async_copy(index_vmem, index_ref, index_sem)
    index_copy.start()
    row = jnp.sum(received_ref[:, 2 * capacity :], axis=0, keepdims=True)
    high, rest = split(row)
    low, _ = split(row - high.astype(jnp.float32) - rest.astype(jnp.float32))
    terms = [high.astype(jnp.float32), rest.astype(jnp.float32), low.astype(jnp.float32)]
    tail = jnp.concatenate(terms + [jnp.zeros((TAIL - 3, features), jnp.float32)], axis=0).astype(jnp.bfloat16)
    for part, copy in enumerate(copies):
        copy.wait()
        for start in range(part * TABLE_STEP, (part + 1) * TABLE_STEP, 256):
            wide_ref[start : start + 256, :] = table_ref[start : start + 256, :].astype(jnp.float32)
    index_copy.wait()

    def one(device, carry):
        rows = [wide_ref[pl.ds(index_ref[device, slot], 1), :] for slot in range(capacity)]
        out_ref[device, :capacity, :] = jnp.concatenate(rows, axis=0).astype(jnp.bfloat16)
        out_ref[device, capacity:, :] = tail
        return carry

    lax.fori_loop(0, devices, one, 0, unroll=FETCH_UNROLL)


def fetch_rows(received, item_table, capacity):
    devices = received.shape[0]
    items, features = item_table.shape
    vmem = pl.BlockSpec(memory_space=pltpu.VMEM)
    return pl.pallas_call(
        fetch_kernel,
        out_shape=jax.ShapeDtypeStruct((devices, capacity + TAIL, features), jnp.bfloat16),
        in_specs=[vmem, pl.BlockSpec(memory_space=pl.ANY)],
        out_specs=vmem,
        scratch_shapes=[
            pltpu.VMEM((items, features), jnp.bfloat16),
            pltpu.VMEM((items, features), jnp.float32),
            pltpu.VMEM((devices, 2 * capacity), jnp.int32),
            pltpu.SMEM((devices, 2 * capacity), jnp.int32),
            pltpu.SemaphoreType.DMA((items // TABLE_STEP,)),
            pltpu.SemaphoreType.DMA,
        ],
        compiler_params=pltpu.CompilerParams(vmem_limit_bytes=VMEM_LIMIT),
        cost_estimate=pl.CostEstimate(flops=0, bytes_accessed=24 * 2**20, transcendentals=0),
    )(received, item_table)


def split(value):
    high = value.astype(jnp.bfloat16)
    low = (value - high.astype(jnp.float32)).astype(jnp.bfloat16)
    return high, low


def solve_kernel(
    total_items, slots_ref, arrived_ref, weights_ref, counts_ref, start_ref, out_ref, wide_ref, shared_ref, conf_ref, system_ref
):
    users, links = slots_ref.shape
    devices, held, features = arrived_ref.shape
    capacity = held - TAIL

    def widen(device, carry):
        start = pl.multiple_of(device * capacity, capacity)
        wide_ref[pl.ds(start, capacity), :] = arrived_ref[device, :capacity, :].astype(jnp.float32)
        tail = arrived_ref[device, capacity:, :].astype(jnp.float32)
        shared_ref[pl.ds(device, 1), :] = jnp.sum(tail, axis=0, keepdims=True)
        return carry

    lax.fori_loop(0, devices, widen, 0, unroll=8)
    diagonal = jnp.where(
        lax.broadcasted_iota(jnp.int32, (features, features), 0)
        == lax.broadcasted_iota(jnp.int32, (features, features), 1),
        0.5 * links,
        0.0,
    )
    shared_ref[...] = shared_ref[...] * (links / total_items) + diagonal
    link_id = lax.broadcasted_iota(jnp.int32, (users, links), 1)
    conf_ref[...] = jnp.where(
        link_id < counts_ref[...], 1.0 + weights_ref[...].astype(jnp.float32) / 8.0, 0.0
    )
    lane = lax.broadcasted_iota(jnp.int32, (features, 2 * users), 1)
    user_lane = jnp.where(lane < users, lane, lane - users)
    ones = jnp.ones((links, 2 * users), jnp.bfloat16)

    def stationary(vector):
        high, low = split(vector)
        half = jnp.where(lane < users, high.astype(jnp.float32), low.astype(jnp.float32)).astype(jnp.bfloat16)
        return jnp.concatenate([half, half], axis=0)

    def both_halves(image):
        return image + pltpu.roll(image, users, 1)

    def form(user, operand, target, image):
        rows = [wide_ref[pl.ds(slots_ref[user, link], 1), :] for link in range(links)]
        fetched = jnp.concatenate(rows, axis=0)
        scaled = (fetched.T * conf_ref[user : user + 1, :]).astype(jnp.bfloat16)
        both = jnp.dot(
            scaled,
            jnp.concatenate([fetched.astype(jnp.bfloat16), ones], axis=1),
            preferred_element_type=jnp.float32,
        )
        system = jnp.concatenate(split(both[:, :features] + shared_ref[...]), axis=1)
        system_ref[user * features : (user + 1) * features, :] = system
        first = jnp.dot(system, operand, preferred_element_type=jnp.float32)
        mine = user_lane == user
        return jnp.where(mine, both[:, features:], target), jnp.where(mine, first, image)

    def apply_system(vector, first, last):
        operand = stationary(vector)
        image = jnp.zeros_like(vector)
        for user in range(first, last, TOGETHER):
            product = jnp.dot(
                system_ref[user * features : (user + TOGETHER) * features, :],
                operand,
                preferred_element_type=jnp.float32,
            )
            for one in range(TOGETHER):
                piece = product[one * features : (one + 1) * features]
                image = jnp.where(user_lane == user + one, piece, image)
        return both_halves(image)

    def refine(first, last, target, image, estimate):
        residual = target - both_halves(image)
        direction = residual
        norm_now = jnp.sum(residual * residual, axis=0, keepdims=True)
        for iteration in range(CG_STEPS):
            image = apply_system(direction, first, last)
            curvature = jnp.sum(direction * image, axis=0, keepdims=True)
            step_len = norm_now / (curvature + 1e-06)
            estimate = estimate + step_len * direction
            residual = residual - step_len * image
            norm_next = jnp.sum(residual * residual, axis=0, keepdims=True)
            direction = residual + norm_next / (norm_now + 1e-06) * direction
            norm_now = norm_next
        return estimate

    start_rows = start_ref[...]
    estimate = jnp.concatenate([start_rows, start_rows], axis=0).T
    operand = stationary(estimate)
    zero = jnp.zeros((features, 2 * users), jnp.float32)
    waiting = None
    for first in range(0, users, BATCH):
        target, image = zero, zero
        for user in range(first, first + BATCH):
            target, image = form(user, operand, target, image)
        if waiting is not None:
            estimate = refine(*waiting, estimate)
        waiting = (first, first + BATCH, target, image)
    out_ref[...] = refine(*waiting, estimate).T[:users]


def solve_rows(link_slots, arrived, link_weights, link_counts, user_rows, total_items):
    users, links = link_slots.shape
    features = user_rows.shape[1]
    vmem = pl.BlockSpec(memory_space=pltpu.VMEM)
    return pl.pallas_call(
        functools.partial(solve_kernel, total_items),
        out_shape=jax.ShapeDtypeStruct((users, features), jnp.float32),
        in_specs=[pl.BlockSpec(memory_space=pltpu.SMEM)] + [vmem] * 4,
        out_specs=vmem,
        scratch_shapes=[
            pltpu.VMEM((users * links, features), jnp.float32),
            pltpu.VMEM((features, features), jnp.float32),
            pltpu.VMEM((users, links), jnp.float32),
            pltpu.VMEM((users * features, 2 * features), jnp.bfloat16),
        ],
        compiler_params=pltpu.CompilerParams(vmem_limit_bytes=VMEM_LIMIT),
        cost_estimate=pl.CostEstimate(flops=2**32, bytes_accessed=24 * 2**20, transcendentals=0),
    )(link_slots, arrived, link_weights, link_counts.reshape(users, 1), user_rows)


def exchange(value):
    return lax.all_to_all(value, AXES, split_axis=0, concat_axis=0, tiled=True)


def per_device(item_table, user_rows, link_rows, link_slots, link_weights, link_counts):
    users, features = user_rows.shape
    links = link_rows.shape[1]
    devices = lax.axis_size("rows") * lax.axis_size("table")
    capacity = users * links // devices
    total_items = item_table.shape[0] * devices
    received = exchange(ask(link_slots, link_rows, item_table, devices))
    arrived = exchange(fetch_rows(received, item_table, capacity))
    return solve_rows(link_slots, arrived, link_weights, link_counts, user_rows, total_items)


def solution(mesh):
    placed = (P(AXES, None),) * 5 + (P(AXES),)
    return jax.shard_map(
        per_device,
        mesh=mesh,
        in_specs=placed,
        out_specs=P(AXES, None),
        check_vma=False,
    )
```

```python
import functools

import jax
import jax.numpy as jnp
from jax import lax
from jax.experimental import pallas as pl
from jax.experimental.pallas import tpu as pltpu
from jax.sharding import PartitionSpec as P

CG_STEPS = 3
BATCHES = (32, 32)
TOGETHER = 4
AXES = ("rows", "table")
VMEM_LIMIT = 60 * 2**20
SOLVE_LIMIT = 24 * 2**20
NT = (((1,), (1,)), ((), ()))
TN = (((0,), (0,)), ((), ()))
TABLE_STEP = 2048
OUT_STEP = 16
PLACE_FIRST = 32
TAIL = 8


def ask_kernel(slots_hbm, rows_hbm, table_hbm, out_ref, slots_ref, rows_ref, table_ref, sems):
    half = table_ref.shape[0] // 2
    copies = [
        pltpu.make_async_copy(source, target, sems.at[at])
        for at, (source, target) in enumerate(
            (
                (slots_hbm, slots_ref),
                (rows_hbm, rows_ref),
                (table_hbm.at[pl.ds(0, half)], table_ref.at[pl.ds(0, half)]),
                (table_hbm.at[pl.ds(half, half)], table_ref.at[pl.ds(half, half)]),
            )
        )
    ]
    for copy in copies:
        copy.start()
    users, links = slots_ref.shape
    devices = out_ref.shape[0]
    items, features = table_ref.shape
    capacity = users * links // devices
    owner_id = lax.broadcasted_iota(jnp.int32, (devices, links), 0)
    lane_id = lax.broadcasted_iota(jnp.int32, (2 * capacity, links), 0)
    upper = lane_id < capacity
    slot_id = jnp.where(upper, lane_id, lane_id - capacity)
    copies[0].wait()
    copies[1].wait()

    def place(user, total):
        owners, named = [], []
        for one in (user, user + 1):
            slots = slots_ref[one : one + 1, :]
            rows = rows_ref[one : one + 1, :]
            owner = slots // capacity
            place = slots - owner * capacity
            high = (rows // 128).astype(jnp.float32)
            low = (rows % 128).astype(jnp.float32)
            owners.append(jnp.where(owner_id == owner, 1.0, 0.0).astype(jnp.bfloat16))
            value = jnp.where(upper, high, low)
            named.append(jnp.where(slot_id == place, value, 0.0).astype(jnp.bfloat16))
        return total + lax.dot_general(
            jnp.concatenate(owners, axis=1),
            jnp.concatenate(named, axis=1),
            NT,
            preferred_element_type=jnp.float32,
        )

    def add_items(start, gramian):
        block = table_ref[start : start + TABLE_STEP, :]
        return gramian + lax.dot_general(block, block, TN, preferred_element_type=jnp.float32)

    total = jnp.zeros((devices, 2 * capacity), jnp.float32)
    gramian = jnp.zeros((features, features), jnp.float32)
    early = PLACE_FIRST
    for user in range(0, early, 2):
        total = place(user, total)
    copies[2].wait()
    starts = list(range(0, half, TABLE_STEP))
    for user in range(early, users, 2):
        total = place(user, total)
        if starts and (user - early) % 8 == 0:
            gramian = add_items(starts.pop(0), gramian)
    for start in starts:
        gramian = add_items(start, gramian)
    asked = total * 128.0 + pltpu.roll(total, capacity, 1)
    lane = lax.broadcasted_iota(jnp.int32, asked.shape, 1)
    out_ref[:, 0, : 2 * capacity] = jnp.where(lane < capacity, asked, 0.0)
    copies[3].wait()
    for start in range(half, items, TABLE_STEP):
        gramian = add_items(start, gramian)
    out_ref[:, 0, 2 * capacity :] = gramian


def ask(link_slots, link_rows, item_table, devices):
    users, links = link_slots.shape
    features = item_table.shape[1]
    capacity = users * links // devices
    return pl.pallas_call(
        ask_kernel,
        out_shape=jax.ShapeDtypeStruct((devices, 1, 2 * capacity + features), jnp.float32),
        in_specs=[pl.BlockSpec(memory_space=pl.ANY)] * 3,
        out_specs=pl.BlockSpec(memory_space=pltpu.VMEM),
        scratch_shapes=[
            pltpu.VMEM(link_slots.shape, jnp.int32),
            pltpu.VMEM(link_rows.shape, jnp.int32),
            pltpu.VMEM(item_table.shape, jnp.bfloat16),
            pltpu.SemaphoreType.DMA((4,)),
        ],
        compiler_params=pltpu.CompilerParams(vmem_limit_bytes=VMEM_LIMIT),
        cost_estimate=pl.CostEstimate(flops=2**30, bytes_accessed=2**22, transcendentals=0),
    )(link_slots, link_rows, item_table)


def fetch_kernel(
    received_ref, table_hbm, out_hbm, table_ref, wide_ref, index_vmem, index_ref, out_ref, table_sems, index_sem, out_sems
):
    items, features = table_ref.shape
    devices, held, _ = out_ref.shape
    capacity = held - TAIL
    parts = items // TABLE_STEP
    copies = []
    for part in range(parts):
        span = pl.ds(part * TABLE_STEP, TABLE_STEP)
        copies.append(pltpu.make_async_copy(table_hbm.at[span], table_ref.at[span], table_sems.at[part]))
        copies[-1].start()
    index_vmem[...] = received_ref[:, 0, : 2 * capacity].astype(jnp.int32)
    index_copy = pltpu.make_async_copy(index_vmem, index_ref, index_sem)
    index_copy.start()
    row = jnp.sum(received_ref[:, 0, 2 * capacity :], axis=0, keepdims=True)
    high, rest = split(row)
    low, _ = split(row - high.astype(jnp.float32) - rest.astype(jnp.float32))
    terms = [high.astype(jnp.float32), rest.astype(jnp.float32), low.astype(jnp.float32)]
    tail = jnp.concatenate(terms + [jnp.zeros((TAIL - 3, features), jnp.float32)], axis=0).astype(jnp.bfloat16)
    for part, copy in enumerate(copies):
        copy.wait()
        for start in range(part * TABLE_STEP, (part + 1) * TABLE_STEP, 256):
            wide_ref[start : start + 256, :] = table_ref[start : start + 256, :].astype(jnp.float32)
    index_copy.wait()

    sent = []
    for device in range(devices):
        rows = [wide_ref[pl.ds(index_ref[device, slot], 1), :] for slot in range(capacity)]
        out_ref[device, :capacity, :] = jnp.concatenate(rows, axis=0).astype(jnp.bfloat16)
        out_ref[device, capacity:, :] = tail
        if (device + 1) % OUT_STEP == 0:
            span = pl.ds(device + 1 - OUT_STEP, OUT_STEP)
            sent.append(pltpu.make_async_copy(out_ref.at[span], out_hbm.at[span], out_sems.at[len(sent)]))
            sent[-1].start()
    for copy in sent:
        copy.wait()


def fetch_rows(received, item_table, capacity):
    devices = received.shape[0]
    items, features = item_table.shape
    vmem = pl.BlockSpec(memory_space=pltpu.VMEM)
    return pl.pallas_call(
        fetch_kernel,
        out_shape=jax.ShapeDtypeStruct((devices, capacity + TAIL, features), jnp.bfloat16),
        in_specs=[vmem, pl.BlockSpec(memory_space=pl.ANY)],
        out_specs=pl.BlockSpec(memory_space=pl.ANY),
        scratch_shapes=[
            pltpu.VMEM((items, features), jnp.bfloat16),
            pltpu.VMEM((items, features), jnp.float32),
            pltpu.VMEM((devices, 2 * capacity), jnp.int32),
            pltpu.SMEM((devices, 2 * capacity), jnp.int32),
            pltpu.VMEM((devices, capacity + TAIL, features), jnp.bfloat16),
            pltpu.SemaphoreType.DMA((items // TABLE_STEP,)),
            pltpu.SemaphoreType.DMA,
            pltpu.SemaphoreType.DMA((devices // OUT_STEP,)),
        ],
        compiler_params=pltpu.CompilerParams(vmem_limit_bytes=VMEM_LIMIT),
        cost_estimate=pl.CostEstimate(flops=0, bytes_accessed=24 * 2**20, transcendentals=0),
    )(received, item_table)


def split(value):
    high = value.astype(jnp.bfloat16)
    low = (value - high.astype(jnp.float32)).astype(jnp.bfloat16)
    return high, low


def solve_kernel(
    total_items, slots_ref, arrived_ref, weights_ref, counts_ref, start_ref, out_ref, wide_ref, shared_ref, conf_ref, system_ref
):
    users, links = slots_ref.shape
    devices, held, features = arrived_ref.shape
    capacity = held - TAIL

    def widen(device, carry):
        start = pl.multiple_of(device * capacity, capacity)
        wide_ref[pl.ds(start, capacity), :] = arrived_ref[device, :capacity, :].astype(jnp.float32)
        tail = arrived_ref[device, capacity:, :].astype(jnp.float32)
        shared_ref[pl.ds(device, 1), :] = jnp.sum(tail, axis=0, keepdims=True)
        return carry

    lax.fori_loop(0, devices, widen, 0, unroll=8)
    diagonal = jnp.where(
        lax.broadcasted_iota(jnp.int32, (features, features), 0)
        == lax.broadcasted_iota(jnp.int32, (features, features), 1),
        0.5 * links,
        0.0,
    )
    shared_ref[...] = shared_ref[...] * (links / total_items) + diagonal
    link_id = lax.broadcasted_iota(jnp.int32, (users, links), 1)
    conf_ref[...] = jnp.where(
        link_id < counts_ref[...], 1.0 + weights_ref[...].astype(jnp.float32) / 8.0, 0.0
    )
    lane = lax.broadcasted_iota(jnp.int32, (features, 2 * users), 1)
    user_lane = jnp.where(lane < users, lane, lane - users)
    ones = jnp.ones((links, 2 * users), jnp.bfloat16)

    def stationary(vector):
        high, low = split(vector)
        half = jnp.where(lane < users, high.astype(jnp.float32), low.astype(jnp.float32)).astype(jnp.bfloat16)
        return jnp.concatenate([half, half], axis=0)

    def both_halves(image):
        return image + pltpu.roll(image, users, 1)

    def form(user, operand, target, image):
        rows = [wide_ref[pl.ds(slots_ref[user, link], 1), :] for link in range(links)]
        fetched = jnp.concatenate(rows, axis=0)
        scaled = (fetched.T * conf_ref[user : user + 1, :]).astype(jnp.bfloat16)
        both = jnp.dot(
            scaled,
            jnp.concatenate([fetched.astype(jnp.bfloat16), ones], axis=1),
            preferred_element_type=jnp.float32,
        )
        system = jnp.concatenate(split(both[:, :features] + shared_ref[...]), axis=1)
        system_ref[user * features : (user + 1) * features, :] = system
        first = jnp.dot(system, operand, preferred_element_type=jnp.float32)
        mine = user_lane == user
        return jnp.where(mine, both[:, features:], target), jnp.where(mine, first, image)

    def refine(first, last, target, image, estimate):
        residual = target - both_halves(image)
        direction = residual
        norm_now = jnp.sum(residual * residual, axis=0, keepdims=True)
        for iteration in range(CG_STEPS):
            operand = stationary(direction)
            image = jnp.zeros_like(direction)
            for user in range(first, last, TOGETHER):
                product = jnp.dot(
                    system_ref[user * features : (user + TOGETHER) * features, :],
                    operand,
                    preferred_element_type=jnp.float32,
                )
                for one in range(TOGETHER):
                    piece = product[one * features : (one + 1) * features]
                    image = jnp.where(user_lane == user + one, piece, image)
            yield None
            image = both_halves(image)
            curvature = jnp.sum(direction * image, axis=0, keepdims=True)
            step_len = norm_now / (curvature + 1e-06)
            estimate = estimate + step_len * direction
            residual = residual - step_len * image
            norm_next = jnp.sum(residual * residual, axis=0, keepdims=True)
            direction = residual + norm_next / (norm_now + 1e-06) * direction
            norm_now = norm_next
        yield estimate

    start_rows = start_ref[...]
    estimate = jnp.concatenate([start_rows, start_rows], axis=0).T
    operand = stationary(estimate)
    zero = jnp.zeros((features, 2 * users), jnp.float32)
    chains, last = [], 0
    for batch in BATCHES:
        first, last = last, last + batch
        target, image = zero, zero
        for user in range(first, last):
            target, image = form(user, operand, target, image)
        chains.append(refine(first, last, target, image, estimate if not chains else zero))
    total = zero
    for _ in range(CG_STEPS + 1):
        done = [next(chain) for chain in chains]
    for one in done:
        total = total + one
    out_ref[...] = total.T[:users]


def solve_rows(link_slots, arrived, link_weights, link_counts, user_rows, total_items):
    users, links = link_slots.shape
    features = user_rows.shape[1]
    vmem = pl.BlockSpec(memory_space=pltpu.VMEM)
    return pl.pallas_call(
        functools.partial(solve_kernel, total_items),
        out_shape=jax.ShapeDtypeStruct((users, features), jnp.float32),
        in_specs=[pl.BlockSpec(memory_space=pltpu.SMEM)] + [vmem] * 4,
        out_specs=vmem,
        scratch_shapes=[
            pltpu.VMEM((users * links, features), jnp.float32),
            pltpu.VMEM((features, features), jnp.float32),
            pltpu.VMEM((users, links), jnp.float32),
            pltpu.VMEM((users * features, 2 * features), jnp.bfloat16),
        ],
        compiler_params=pltpu.CompilerParams(vmem_limit_bytes=SOLVE_LIMIT),
        cost_estimate=pl.CostEstimate(flops=2**32, bytes_accessed=24 * 2**20, transcendentals=0),
    )(link_slots, arrived, link_weights, link_counts.reshape(users, 1), user_rows)


def exchange(value):
    return lax.all_to_all(value, AXES, split_axis=0, concat_axis=0, tiled=True)


def per_device(item_table, user_rows, link_rows, link_slots, link_weights, link_counts):
    users, features = user_rows.shape
    links = link_rows.shape[1]
    devices = lax.axis_size("rows") * lax.axis_size("table")
    capacity = users * links // devices
    total_items = item_table.shape[0] * devices
    received = exchange(ask(link_slots, link_rows, item_table, devices))
    arrived = exchange(fetch_rows(received, item_table, capacity))
    return solve_rows(link_slots, arrived, link_weights, link_counts, user_rows, total_items)


def solution(mesh):
    placed = (P(AXES, None),) * 5 + (P(AXES),)
    return jax.shard_map(
        per_device,
        mesh=mesh,
        in_specs=placed,
        out_specs=P(AXES, None),
        check_vma=False,
    )
```

```python
import functools

import jax
import jax.numpy as jnp
from jax import lax
from jax.experimental import pallas as pl
from jax.experimental.pallas import tpu as pltpu
from jax.sharding import PartitionSpec as P

CG_STEPS = 3
BATCHES = (32, 32)
TOGETHER = 4
AXES = ("rows", "table")
VMEM_LIMIT = 56 * 2**20
FETCH_LIMIT = 24 * 2**20
SOLVE_LIMIT = 24 * 2**20
NT = (((1,), (1,)), ((), ()))
TN = (((0,), (0,)), ((), ()))
TABLE_STEP = 2048
OUT_STEP = 8
INDEX_PIECES = 4
PLACE_FIRST = 32
TAIL = 8


def ask_kernel(slots_hbm, rows_hbm, table_hbm, out_ref, slots_ref, rows_ref, table_ref, sems):
    half = table_ref.shape[0] // 2
    copies = [
        pltpu.make_async_copy(source, target, sems.at[at])
        for at, (source, target) in enumerate(
            (
                (slots_hbm, slots_ref),
                (rows_hbm, rows_ref),
                (table_hbm.at[pl.ds(0, half)], table_ref.at[pl.ds(0, half)]),
                (table_hbm.at[pl.ds(half, half)], table_ref.at[pl.ds(half, half)]),
            )
        )
    ]
    for copy in copies:
        copy.start()
    users, links = slots_ref.shape
    devices = out_ref.shape[0]
    items, features = table_ref.shape
    capacity = users * links // devices
    owner_id = lax.broadcasted_iota(jnp.int32, (devices, links), 0)
    lane_id = lax.broadcasted_iota(jnp.int32, (2 * capacity, links), 0)
    upper = lane_id < capacity
    slot_id = jnp.where(upper, lane_id, lane_id - capacity)
    copies[0].wait()
    copies[1].wait()

    def place(user, total):
        owners, named = [], []
        for one in (user, user + 1):
            slots = slots_ref[one : one + 1, :]
            rows = rows_ref[one : one + 1, :]
            owner = slots // capacity
            place = slots - owner * capacity
            high = (rows // 128).astype(jnp.float32)
            low = (rows % 128).astype(jnp.float32)
            owners.append(jnp.where(owner_id == owner, 1.0, 0.0).astype(jnp.bfloat16))
            value = jnp.where(upper, high, low)
            named.append(jnp.where(slot_id == place, value, 0.0).astype(jnp.bfloat16))
        return total + lax.dot_general(
            jnp.concatenate(owners, axis=1),
            jnp.concatenate(named, axis=1),
            NT,
            preferred_element_type=jnp.float32,
        )

    def add_items(start, gramian):
        block = table_ref[start : start + TABLE_STEP, :]
        return gramian + lax.dot_general(block, block, TN, preferred_element_type=jnp.float32)

    total = jnp.zeros((devices, 2 * capacity), jnp.float32)
    gramian = jnp.zeros((features, features), jnp.float32)
    early = PLACE_FIRST
    for user in range(0, early, 2):
        total = place(user, total)
    copies[2].wait()
    starts = list(range(0, half, TABLE_STEP))
    for user in range(early, users, 2):
        total = place(user, total)
        if starts and (user - early) % 8 == 0:
            gramian = add_items(starts.pop(0), gramian)
    for start in starts:
        gramian = add_items(start, gramian)
    asked = total * 128.0 + pltpu.roll(total, capacity, 1)
    lane = lax.broadcasted_iota(jnp.int32, asked.shape, 1)
    out_ref[:, 0, : 2 * capacity] = jnp.where(lane < capacity, asked, 0.0)
    copies[3].wait()
    for start in range(half, items, TABLE_STEP):
        gramian = add_items(start, gramian)
    out_ref[:, 0, 2 * capacity :] = gramian


def ask(link_slots, link_rows, item_table, devices):
    users, links = link_slots.shape
    features = item_table.shape[1]
    capacity = users * links // devices
    return pl.pallas_call(
        ask_kernel,
        out_shape=jax.ShapeDtypeStruct((devices, 1, 2 * capacity + features), jnp.float32),
        in_specs=[pl.BlockSpec(memory_space=pl.ANY)] * 3,
        out_specs=pl.BlockSpec(memory_space=pltpu.VMEM),
        scratch_shapes=[
            pltpu.VMEM(link_slots.shape, jnp.int32),
            pltpu.VMEM(link_rows.shape, jnp.int32),
            pltpu.VMEM(item_table.shape, jnp.bfloat16),
            pltpu.SemaphoreType.DMA((4,)),
        ],
        compiler_params=pltpu.CompilerParams(vmem_limit_bytes=VMEM_LIMIT),
        cost_estimate=pl.CostEstimate(flops=2**30, bytes_accessed=2**22, transcendentals=0),
    )(link_slots, link_rows, item_table)


def fetch_kernel(received_ref, table_ref, out_hbm, wide_ref, index_vmem, index_ref, out_ref, index_sems, out_sems):
    items, features = table_ref.shape
    devices, held, _ = out_ref.shape
    capacity = held - TAIL
    index = received_ref[:, 0, : 2 * capacity]
    half = devices // 2
    lane = lax.broadcasted_iota(jnp.int32, (half, 2 * capacity), 1)
    index = jnp.where(lane < capacity, index[:half], pltpu.roll(index[half:], capacity, 1))
    index_vmem[...] = index.astype(jnp.int32)
    index_copies = []
    for piece in range(INDEX_PIECES):
        span = pl.ds(piece * (half // INDEX_PIECES), half // INDEX_PIECES)
        index_copies.append(pltpu.make_async_copy(index_vmem.at[span], index_ref.at[span], index_sems.at[piece]))
        index_copies[-1].start()
    row = jnp.sum(received_ref[:, 0, 2 * capacity :], axis=0, keepdims=True)
    high, rest = split(row)
    low, _ = split(row - high.astype(jnp.float32) - rest.astype(jnp.float32))
    terms = [high.astype(jnp.float32), rest.astype(jnp.float32), low.astype(jnp.float32)]
    tail = jnp.concatenate(terms + [jnp.zeros((TAIL - 3, features), jnp.float32)], axis=0).astype(jnp.bfloat16)
    for start in range(0, items, 256):
        wide_ref[start : start + 256, :] = table_ref[start : start + 256, :].astype(jnp.float32)
    sent = []
    for at in range(half):
        if at % (half // INDEX_PIECES) == 0:
            index_copies[at // (half // INDEX_PIECES)].wait()
        for device, place in ((at, 0), (half + at, capacity)):
            rows = [wide_ref[pl.ds(index_ref[at, place + slot], 1), :] for slot in range(capacity)]
            out_ref[device, :capacity, :] = jnp.concatenate(rows, axis=0).astype(jnp.bfloat16)
            out_ref[device, capacity:, :] = tail
        if (at + 1) % OUT_STEP == 0:
            for end in (at + 1, half + at + 1):
                span = pl.ds(end - OUT_STEP, OUT_STEP)
                sent.append(pltpu.make_async_copy(out_ref.at[span], out_hbm.at[span], out_sems.at[len(sent)]))
                sent[-1].start()
    for copy in sent:
        copy.wait()


def fetch_rows(received, item_table, capacity):
    devices = received.shape[0]
    items, features = item_table.shape
    vmem = pl.BlockSpec(memory_space=pltpu.VMEM)
    return pl.pallas_call(
        fetch_kernel,
        out_shape=jax.ShapeDtypeStruct((devices, capacity + TAIL, features), jnp.bfloat16),
        in_specs=[vmem, vmem],
        out_specs=pl.BlockSpec(memory_space=pl.ANY),
        scratch_shapes=[
            pltpu.VMEM((items, features), jnp.float32),
            pltpu.VMEM((devices // 2, 2 * capacity), jnp.int32),
            pltpu.SMEM((devices // 2, 2 * capacity), jnp.int32),
            pltpu.VMEM((devices, capacity + TAIL, features), jnp.bfloat16),
            pltpu.SemaphoreType.DMA((INDEX_PIECES,)),
            pltpu.SemaphoreType.DMA((devices // OUT_STEP,)),
        ],
        compiler_params=pltpu.CompilerParams(vmem_limit_bytes=FETCH_LIMIT),
        cost_estimate=pl.CostEstimate(flops=0, bytes_accessed=24 * 2**20, transcendentals=0),
    )(received, item_table)


def split(value):
    high = value.astype(jnp.bfloat16)
    low = (value - high.astype(jnp.float32)).astype(jnp.bfloat16)
    return high, low


def solve_kernel(
    total_items,
    slots_hbm,
    arrived_ref,
    weights_ref,
    counts_ref,
    start_ref,
    out_ref,
    wide_ref,
    shared_ref,
    conf_ref,
    system_ref,
    slots_ref,
    slots_sem,
):
    users, links = slots_ref.shape
    devices, held, features = arrived_ref.shape
    slots_copy = pltpu.make_async_copy(slots_hbm, slots_ref, slots_sem)
    slots_copy.start()
    capacity = held - TAIL

    def widen(device, carry):
        start = pl.multiple_of(device * capacity, capacity)
        wide_ref[pl.ds(start, capacity), :] = arrived_ref[device, :capacity, :].astype(jnp.float32)
        tail = arrived_ref[device, capacity:, :].astype(jnp.float32)
        shared_ref[pl.ds(device, 1), :] = jnp.sum(tail, axis=0, keepdims=True)
        return carry

    lax.fori_loop(0, devices, widen, 0, unroll=8)
    diagonal = jnp.where(
        lax.broadcasted_iota(jnp.int32, (features, features), 0)
        == lax.broadcasted_iota(jnp.int32, (features, features), 1),
        0.5 * links,
        0.0,
    )
    shared_ref[...] = shared_ref[...] * (links / total_items) + diagonal
    link_id = lax.broadcasted_iota(jnp.int32, (users, links), 1)
    conf_ref[...] = jnp.where(
        link_id < counts_ref[...], 1.0 + weights_ref[...].astype(jnp.float32) / 8.0, 0.0
    )
    lane = lax.broadcasted_iota(jnp.int32, (features, 2 * users), 1)
    user_lane = jnp.where(lane < users, lane, lane - users)
    ones = jnp.ones((links, 2 * users), jnp.bfloat16)

    def stationary(vector):
        high, low = split(vector)
        half = jnp.where(lane < users, high.astype(jnp.float32), low.astype(jnp.float32)).astype(jnp.bfloat16)
        return jnp.concatenate([half, half], axis=0)

    def both_halves(image):
        return image + pltpu.roll(image, users, 1)

    def form(user, operand, target, image):
        rows = [wide_ref[pl.ds(slots_ref[user, link], 1), :] for link in range(links)]
        fetched = jnp.concatenate(rows, axis=0)
        scaled = (fetched.T * conf_ref[user : user + 1, :]).astype(jnp.bfloat16)
        both = jnp.dot(
            scaled,
            jnp.concatenate([fetched.astype(jnp.bfloat16), ones], axis=1),
            preferred_element_type=jnp.float32,
        )
        system = jnp.concatenate(split(both[:, :features] + shared_ref[...]), axis=1)
        system_ref[user * features : (user + 1) * features, :] = system
        first = jnp.dot(system, operand, preferred_element_type=jnp.float32)
        mine = user_lane == user
        return jnp.where(mine, both[:, features:], target), jnp.where(mine, first, image)

    def refine(first, last, target, image, estimate):
        residual = target - both_halves(image)
        direction = residual
        norm_now = jnp.sum(residual * residual, axis=0, keepdims=True)
        for iteration in range(CG_STEPS):
            operand = stationary(direction)
            image = jnp.zeros_like(direction)
            for user in range(first, last, TOGETHER):
                product = jnp.dot(
                    system_ref[user * features : (user + TOGETHER) * features, :],
                    operand,
                    preferred_element_type=jnp.float32,
                )
                for one in range(TOGETHER):
                    piece = product[one * features : (one + 1) * features]
                    image = jnp.where(user_lane == user + one, piece, image)
            yield None
            image = both_halves(image)
            curvature = jnp.sum(direction * image, axis=0, keepdims=True)
            step_len = norm_now / (curvature + 1e-06)
            estimate = estimate + step_len * direction
            residual = residual - step_len * image
            norm_next = jnp.sum(residual * residual, axis=0, keepdims=True)
            direction = residual + norm_next / (norm_now + 1e-06) * direction
            norm_now = norm_next
        yield estimate

    start_rows = start_ref[...]
    estimate = jnp.concatenate([start_rows, start_rows], axis=0).T
    operand = stationary(estimate)
    zero = jnp.zeros((features, 2 * users), jnp.float32)
    slots_copy.wait()
    chains, last = [], 0
    for batch in BATCHES:
        first, last = last, last + batch
        target, image = zero, zero
        for user in range(first, last):
            target, image = form(user, operand, target, image)
        chains.append(refine(first, last, target, image, estimate if not chains else zero))
    total = zero
    for _ in range(CG_STEPS + 1):
        done = [next(chain) for chain in chains]
    for one in done:
        total = total + one
    out_ref[...] = total.T[:users]


def solve_rows(link_slots, arrived, link_weights, link_counts, user_rows, total_items):
    users, links = link_slots.shape
    features = user_rows.shape[1]
    vmem = pl.BlockSpec(memory_space=pltpu.VMEM)
    return pl.pallas_call(
        functools.partial(solve_kernel, total_items),
        out_shape=jax.ShapeDtypeStruct((users, features), jnp.float32),
        in_specs=[pl.BlockSpec(memory_space=pl.ANY)] + [vmem] * 4,
        out_specs=vmem,
        scratch_shapes=[
            pltpu.VMEM((users * links, features), jnp.float32),
            pltpu.VMEM((features, features), jnp.float32),
            pltpu.VMEM((users, links), jnp.float32),
            pltpu.VMEM((users * features, 2 * features), jnp.bfloat16),
            pltpu.SMEM((users, links), jnp.int32),
            pltpu.SemaphoreType.DMA,
        ],
        compiler_params=pltpu.CompilerParams(vmem_limit_bytes=SOLVE_LIMIT),
        cost_estimate=pl.CostEstimate(flops=2**32, bytes_accessed=24 * 2**20, transcendentals=0),
    )(link_slots, arrived, link_weights, link_counts.reshape(users, 1), user_rows)


def exchange(value):
    return lax.all_to_all(value, AXES, split_axis=0, concat_axis=0, tiled=True)


def per_device(item_table, user_rows, link_rows, link_slots, link_weights, link_counts):
    users, features = user_rows.shape
    links = link_rows.shape[1]
    devices = lax.axis_size("rows") * lax.axis_size("table")
    capacity = users * links // devices
    total_items = item_table.shape[0] * devices
    received = exchange(ask(link_slots, link_rows, item_table, devices))
    arrived = exchange(fetch_rows(received, item_table, capacity))
    return solve_rows(link_slots, arrived, link_weights, link_counts, user_rows, total_items)


def solution(mesh):
    placed = (P(AXES, None),) * 5 + (P(AXES),)
    return jax.shard_map(
        per_device,
        mesh=mesh,
        in_specs=placed,
        out_specs=P(AXES, None),
        check_vma=False,
    )
```

```python
import functools

import jax
import jax.numpy as jnp
from jax import lax
from jax.experimental import pallas as pl
from jax.experimental.pallas import tpu as pltpu
from jax.sharding import PartitionSpec as P

CG_STEPS = 3
BATCHES = (32, 32)
TOGETHER = 8
FORMED = 16
AXES = ("rows", "table")
VMEM_LIMIT = 56 * 2**20
FETCH_LIMIT = 24 * 2**20
SOLVE_LIMIT = 24 * 2**20
NT = (((1,), (1,)), ((), ()))
TN = (((0,), (0,)), ((), ()))
TABLE_STEP = 2048
OUT_STEP = 8
INDEX_PIECES = 4
PLACE_FIRST = 32
TAIL = 8


def ask_kernel(slots_hbm, rows_hbm, table_hbm, out_ref, slots_ref, rows_ref, table_ref, sems):
    half = table_ref.shape[0] // 2
    copies = [
        pltpu.make_async_copy(source, target, sems.at[at])
        for at, (source, target) in enumerate(
            (
                (slots_hbm, slots_ref),
                (rows_hbm, rows_ref),
                (table_hbm.at[pl.ds(0, half)], table_ref.at[pl.ds(0, half)]),
                (table_hbm.at[pl.ds(half, half)], table_ref.at[pl.ds(half, half)]),
            )
        )
    ]
    for copy in copies:
        copy.start()
    users, links = slots_ref.shape
    devices = out_ref.shape[0]
    items, features = table_ref.shape
    capacity = users * links // devices
    owner_id = lax.broadcasted_iota(jnp.int32, (devices, links), 0)
    lane_id = lax.broadcasted_iota(jnp.int32, (2 * capacity, links), 0)
    upper = lane_id < capacity
    slot_id = jnp.where(upper, lane_id, lane_id - capacity)
    copies[0].wait()
    copies[1].wait()

    def place(user, total):
        owners, named = [], []
        for one in (user, user + 1):
            slots = slots_ref[one : one + 1, :]
            rows = rows_ref[one : one + 1, :]
            owner = slots // capacity
            place = slots - owner * capacity
            high = (rows // 128).astype(jnp.float32)
            low = (rows % 128).astype(jnp.float32)
            owners.append(jnp.where(owner_id == owner, 1.0, 0.0).astype(jnp.bfloat16))
            value = jnp.where(upper, high, low)
            named.append(jnp.where(slot_id == place, value, 0.0).astype(jnp.bfloat16))
        return total + lax.dot_general(
            jnp.concatenate(owners, axis=1),
            jnp.concatenate(named, axis=1),
            NT,
            preferred_element_type=jnp.float32,
        )

    def add_items(start, gramian):
        block = table_ref[start : start + TABLE_STEP, :]
        return gramian + lax.dot_general(block, block, TN, preferred_element_type=jnp.float32)

    total = jnp.zeros((devices, 2 * capacity), jnp.float32)
    gramian = jnp.zeros((features, features), jnp.float32)
    early = PLACE_FIRST
    for user in range(0, early, 2):
        total = place(user, total)
    copies[2].wait()
    starts = list(range(0, half, TABLE_STEP))
    for user in range(early, users, 2):
        total = place(user, total)
        if starts and (user - early) % 8 == 0:
            gramian = add_items(starts.pop(0), gramian)
    for start in starts:
        gramian = add_items(start, gramian)
    asked = total * 128.0 + pltpu.roll(total, capacity, 1)
    lane = lax.broadcasted_iota(jnp.int32, asked.shape, 1)
    out_ref[:, 0, : 2 * capacity] = jnp.where(lane < capacity, asked, 0.0)
    copies[3].wait()
    for start in range(half, items, TABLE_STEP):
        gramian = add_items(start, gramian)
    out_ref[:, 0, 2 * capacity :] = gramian


def ask(link_slots, link_rows, item_table, devices):
    users, links = link_slots.shape
    features = item_table.shape[1]
    capacity = users * links // devices
    return pl.pallas_call(
        ask_kernel,
        out_shape=jax.ShapeDtypeStruct((devices, 1, 2 * capacity + features), jnp.float32),
        in_specs=[pl.BlockSpec(memory_space=pl.ANY)] * 3,
        out_specs=pl.BlockSpec(memory_space=pltpu.VMEM),
        scratch_shapes=[
            pltpu.VMEM(link_slots.shape, jnp.int32),
            pltpu.VMEM(link_rows.shape, jnp.int32),
            pltpu.VMEM(item_table.shape, jnp.bfloat16),
            pltpu.SemaphoreType.DMA((4,)),
        ],
        compiler_params=pltpu.CompilerParams(vmem_limit_bytes=VMEM_LIMIT),
        cost_estimate=pl.CostEstimate(flops=2**30, bytes_accessed=2**22, transcendentals=0),
    )(link_slots, link_rows, item_table)


def fetch_kernel(received_ref, table_ref, out_hbm, wide_ref, index_vmem, index_ref, out_ref, index_sems, out_sems):
    items, features = table_ref.shape
    devices, held, _ = out_ref.shape
    capacity = held - TAIL
    index = received_ref[:, 0, : 2 * capacity]
    half = devices // 2
    lane = lax.broadcasted_iota(jnp.int32, (half, 2 * capacity), 1)
    index = jnp.where(lane < capacity, index[:half], pltpu.roll(index[half:], capacity, 1))
    index_vmem[...] = index.astype(jnp.int32)
    index_copies = []
    for piece in range(INDEX_PIECES):
        span = pl.ds(piece * (half // INDEX_PIECES), half // INDEX_PIECES)
        index_copies.append(pltpu.make_async_copy(index_vmem.at[span], index_ref.at[span], index_sems.at[piece]))
        index_copies[-1].start()
    row = jnp.sum(received_ref[:, 0, 2 * capacity :], axis=0, keepdims=True)
    high, rest = split(row)
    low, _ = split(row - high.astype(jnp.float32) - rest.astype(jnp.float32))
    terms = [high.astype(jnp.float32), rest.astype(jnp.float32), low.astype(jnp.float32)]
    tail = jnp.concatenate(terms + [jnp.zeros((TAIL - 3, features), jnp.float32)], axis=0).astype(jnp.bfloat16)
    for start in range(0, items, 256):
        wide_ref[start : start + 256, :] = table_ref[start : start + 256, :].astype(jnp.float32)
    sent = []
    for at in range(half):
        if at % (half // INDEX_PIECES) == 0:
            index_copies[at // (half // INDEX_PIECES)].wait()
        for device, place in ((at, 0), (half + at, capacity)):
            rows = [wide_ref[pl.ds(index_ref[at, place + slot], 1), :] for slot in range(capacity)]
            out_ref[device, :capacity, :] = jnp.concatenate(rows, axis=0).astype(jnp.bfloat16)
            out_ref[device, capacity:, :] = tail
        if (at + 1) % OUT_STEP == 0:
            for end in (at + 1, half + at + 1):
                span = pl.ds(end - OUT_STEP, OUT_STEP)
                sent.append(pltpu.make_async_copy(out_ref.at[span], out_hbm.at[span], out_sems.at[len(sent)]))
                sent[-1].start()
    for copy in sent:
        copy.wait()


def fetch_rows(received, item_table, capacity):
    devices = received.shape[0]
    items, features = item_table.shape
    vmem = pl.BlockSpec(memory_space=pltpu.VMEM)
    return pl.pallas_call(
        fetch_kernel,
        out_shape=jax.ShapeDtypeStruct((devices, capacity + TAIL, features), jnp.bfloat16),
        in_specs=[vmem, vmem],
        out_specs=pl.BlockSpec(memory_space=pl.ANY),
        scratch_shapes=[
            pltpu.VMEM((items, features), jnp.float32),
            pltpu.VMEM((devices // 2, 2 * capacity), jnp.int32),
            pltpu.SMEM((devices // 2, 2 * capacity), jnp.int32),
            pltpu.VMEM((devices, capacity + TAIL, features), jnp.bfloat16),
            pltpu.SemaphoreType.DMA((INDEX_PIECES,)),
            pltpu.SemaphoreType.DMA((devices // OUT_STEP,)),
        ],
        compiler_params=pltpu.CompilerParams(vmem_limit_bytes=FETCH_LIMIT),
        cost_estimate=pl.CostEstimate(flops=0, bytes_accessed=24 * 2**20, transcendentals=0),
    )(received, item_table)


def split(value):
    high = value.astype(jnp.bfloat16)
    low = (value - high.astype(jnp.float32)).astype(jnp.bfloat16)
    return high, low


def solve_kernel(
    total_items,
    slots_hbm,
    arrived_ref,
    weights_ref,
    counts_ref,
    start_ref,
    out_ref,
    wide_ref,
    shared_ref,
    conf_ref,
    system_ref,
    slots_ref,
    slots_sem,
):
    users, links = slots_ref.shape
    devices, held, features = arrived_ref.shape
    slots_copy = pltpu.make_async_copy(slots_hbm, slots_ref, slots_sem)
    slots_copy.start()
    capacity = held - TAIL

    def widen(device, carry):
        start = pl.multiple_of(device * capacity, capacity)
        wide_ref[pl.ds(start, capacity), :] = arrived_ref[device, :capacity, :].astype(jnp.float32)
        tail = arrived_ref[device, capacity:, :].astype(jnp.float32)
        shared_ref[pl.ds(device, 1), :] = jnp.sum(tail, axis=0, keepdims=True)
        return carry

    lax.fori_loop(0, devices, widen, 0, unroll=8)
    diagonal = jnp.where(
        lax.broadcasted_iota(jnp.int32, (features, features), 0)
        == lax.broadcasted_iota(jnp.int32, (features, features), 1),
        0.5 * links,
        0.0,
    )
    shared_ref[...] = shared_ref[...] * (links / total_items) + diagonal
    link_id = lax.broadcasted_iota(jnp.int32, (users, links), 1)
    conf_ref[...] = jnp.where(
        link_id < counts_ref[...], 1.0 + weights_ref[...].astype(jnp.float32) / 8.0, 0.0
    )
    lane = lax.broadcasted_iota(jnp.int32, (1, 2 * users), 1)
    user_lane = jnp.where(lane < users, lane, lane - users)
    ones = jnp.ones((links, 2 * users), jnp.bfloat16)

    def stationary(vector):
        high, low = split(vector)
        half = jnp.where(lane < users, high.astype(jnp.float32), low.astype(jnp.float32)).astype(jnp.bfloat16)
        return jnp.concatenate([half, half], axis=0)

    def both_halves(image):
        return image + pltpu.roll(image, users, 1)

    def form(user, target):
        rows = [wide_ref[pl.ds(slots_ref[user, link], 1), :] for link in range(links)]
        fetched = jnp.concatenate(rows, axis=0)
        scaled = (fetched.T * conf_ref[user : user + 1, :]).astype(jnp.bfloat16)
        both = jnp.dot(
            scaled,
            jnp.concatenate([fetched.astype(jnp.bfloat16), ones], axis=1),
            preferred_element_type=jnp.float32,
        )
        system = jnp.concatenate(split(both[:, :features] + shared_ref[...]), axis=1)
        system_ref[user * features : (user + 1) * features, :] = system
        return jnp.where(user_lane == user, both[:, features:], target)

    def apply_some(user, count, operand, image):
        product = jnp.dot(
            system_ref[user * features : (user + count) * features, :], operand, preferred_element_type=jnp.float32
        )
        for one in range(count):
            piece = product[one * features : (one + 1) * features]
            image = jnp.where(user_lane == user + one, piece, image)
        return image

    def refine(first, last, target, image, estimate):
        residual = target - both_halves(image)
        direction = residual
        norm_now = jnp.sum(residual * residual, axis=0, keepdims=True)
        for iteration in range(CG_STEPS):
            operand = stationary(direction)
            image = jnp.zeros_like(direction)
            for user in range(first, last, TOGETHER):
                image = apply_some(user, TOGETHER, operand, image)
            yield None
            image = both_halves(image)
            curvature = jnp.sum(direction * image, axis=0, keepdims=True)
            step_len = norm_now / (curvature + 1e-06)
            estimate = estimate + step_len * direction
            residual = residual - step_len * image
            norm_next = jnp.sum(residual * residual, axis=0, keepdims=True)
            direction = residual + norm_next / (norm_now + 1e-06) * direction
            norm_now = norm_next
        yield estimate

    start_rows = start_ref[...]
    estimate = jnp.concatenate([start_rows, start_rows], axis=0).T
    operand = stationary(estimate)
    zero = jnp.zeros((features, 2 * users), jnp.float32)
    slots_copy.wait()
    chains, last = [], 0
    for batch in BATCHES:
        first, last = last, last + batch
        target, image = zero, zero
        for user in range(first, last):
            target = form(user, target)
            if (user + 1) % FORMED == 0:
                image = apply_some(user + 1 - FORMED, FORMED, operand, image)
        chains.append(refine(first, last, target, image, estimate if not chains else zero))
    total = zero
    for _ in range(CG_STEPS + 1):
        done = [next(chain) for chain in chains]
    for one in done:
        total = total + one
    out_ref[...] = total.T[:users]


def solve_rows(link_slots, arrived, link_weights, link_counts, user_rows, total_items):
    users, links = link_slots.shape
    features = user_rows.shape[1]
    vmem = pl.BlockSpec(memory_space=pltpu.VMEM)
    return pl.pallas_call(
        functools.partial(solve_kernel, total_items),
        out_shape=jax.ShapeDtypeStruct((users, features), jnp.float32),
        in_specs=[pl.BlockSpec(memory_space=pl.ANY)] + [vmem] * 4,
        out_specs=vmem,
        scratch_shapes=[
            pltpu.VMEM((users * links, features), jnp.float32),
            pltpu.VMEM((features, features), jnp.float32),
            pltpu.VMEM((users, links), jnp.float32),
            pltpu.VMEM((users * features, 2 * features), jnp.bfloat16),
            pltpu.SMEM((users, links), jnp.int32),
            pltpu.SemaphoreType.DMA,
        ],
        compiler_params=pltpu.CompilerParams(vmem_limit_bytes=SOLVE_LIMIT),
        cost_estimate=pl.CostEstimate(flops=2**32, bytes_accessed=24 * 2**20, transcendentals=0),
    )(link_slots, arrived, link_weights, link_counts.reshape(users, 1), user_rows)


def exchange(value):
    return lax.all_to_all(value, AXES, split_axis=0, concat_axis=0, tiled=True)


def per_device(item_table, user_rows, link_rows, link_slots, link_weights, link_counts):
    users, features = user_rows.shape
    links = link_rows.shape[1]
    devices = lax.axis_size("rows") * lax.axis_size("table")
    capacity = users * links // devices
    total_items = item_table.shape[0] * devices
    received = exchange(ask(link_slots, link_rows, item_table, devices))
    arrived = exchange(fetch_rows(received, item_table, capacity))
    return solve_rows(link_slots, arrived, link_weights, link_counts, user_rows, total_items)


def solution(mesh):
    placed = (P(AXES, None),) * 5 + (P(AXES),)
    return jax.shard_map(
        per_device,
        mesh=mesh,
        in_specs=placed,
        out_specs=P(AXES, None),
        check_vma=False,
    )
```

```python
import functools

import jax
import jax.numpy as jnp
from jax import lax
from jax.experimental import pallas as pl
from jax.experimental.pallas import tpu as pltpu
from jax.sharding import PartitionSpec as P

CG_STEPS = 3
BATCHES = (32, 32)
TOGETHER = 8
FORMED = 16
AXES = ("rows", "table")
VMEM_LIMIT = 56 * 2**20
FETCH_LIMIT = 24 * 2**20
SOLVE_LIMIT = 24 * 2**20
NT = (((1,), (1,)), ((), ()))
TN = (((0,), (0,)), ((), ()))
TABLE_STEP = 2048
INDEX_PIECES = 4
PLACE_FIRST = 32
TAIL = 8


def ask_kernel(slots_hbm, rows_hbm, table_hbm, out_ref, slots_ref, rows_ref, table_ref, sems):
    half = table_ref.shape[0] // 2
    copies = [
        pltpu.make_async_copy(source, target, sems.at[at])
        for at, (source, target) in enumerate(
            (
                (slots_hbm, slots_ref),
                (rows_hbm, rows_ref),
                (table_hbm.at[pl.ds(0, half)], table_ref.at[pl.ds(0, half)]),
                (table_hbm.at[pl.ds(half, half)], table_ref.at[pl.ds(half, half)]),
            )
        )
    ]
    for copy in copies:
        copy.start()
    users, links = slots_ref.shape
    devices = out_ref.shape[0]
    items, features = table_ref.shape
    capacity = users * links // devices
    owner_id = lax.broadcasted_iota(jnp.int32, (devices, links), 0)
    lane_id = lax.broadcasted_iota(jnp.int32, (2 * capacity, links), 0)
    upper = lane_id < capacity
    slot_id = jnp.where(upper, lane_id, lane_id - capacity)
    copies[0].wait()
    copies[1].wait()

    def place(user, total):
        owners, named = [], []
        for one in (user, user + 1):
            slots = slots_ref[one : one + 1, :]
            rows = rows_ref[one : one + 1, :]
            owner = slots // capacity
            place = slots - owner * capacity
            high = (rows // 128).astype(jnp.float32)
            low = (rows % 128).astype(jnp.float32)
            owners.append(jnp.where(owner_id == owner, 1.0, 0.0).astype(jnp.bfloat16))
            value = jnp.where(upper, high, low)
            named.append(jnp.where(slot_id == place, value, 0.0).astype(jnp.bfloat16))
        return total + lax.dot_general(
            jnp.concatenate(owners, axis=1),
            jnp.concatenate(named, axis=1),
            NT,
            preferred_element_type=jnp.float32,
        )

    def add_items(start, gramian):
        block = table_ref[start : start + TABLE_STEP, :]
        return gramian + lax.dot_general(block, block, TN, preferred_element_type=jnp.float32)

    total = jnp.zeros((devices, 2 * capacity), jnp.float32)
    gramian = jnp.zeros((features, features), jnp.float32)
    early = PLACE_FIRST
    for user in range(0, early, 2):
        total = place(user, total)
    copies[2].wait()
    starts = list(range(0, half, TABLE_STEP))
    for user in range(early, users, 2):
        total = place(user, total)
        if starts and (user - early) % 8 == 0:
            gramian = add_items(starts.pop(0), gramian)
    for start in starts:
        gramian = add_items(start, gramian)
    asked = total * 128.0 + pltpu.roll(total, capacity, 1)
    lane = lax.broadcasted_iota(jnp.int32, asked.shape, 1)
    out_ref[:, 0, : 2 * capacity] = jnp.where(lane < capacity, asked, 0.0)
    copies[3].wait()
    for start in range(half, items, TABLE_STEP):
        gramian = add_items(start, gramian)
    out_ref[:, 0, 2 * capacity :] = gramian


def ask(link_slots, link_rows, item_table, devices):
    users, links = link_slots.shape
    features = item_table.shape[1]
    capacity = users * links // devices
    return pl.pallas_call(
        ask_kernel,
        out_shape=jax.ShapeDtypeStruct((devices, 1, 2 * capacity + features), jnp.float32),
        in_specs=[pl.BlockSpec(memory_space=pl.ANY)] * 3,
        out_specs=pl.BlockSpec(memory_space=pltpu.VMEM),
        scratch_shapes=[
            pltpu.VMEM(link_slots.shape, jnp.int32),
            pltpu.VMEM(link_rows.shape, jnp.int32),
            pltpu.VMEM(item_table.shape, jnp.bfloat16),
            pltpu.SemaphoreType.DMA((4,)),
        ],
        compiler_params=pltpu.CompilerParams(vmem_limit_bytes=VMEM_LIMIT),
        cost_estimate=pl.CostEstimate(flops=2**30, bytes_accessed=2**22, transcendentals=0),
    )(link_slots, link_rows, item_table)


def fetch_kernel(received_ref, table_ref, out_ref, wide_ref, index_vmem, index_ref, index_sems):
    items, features = table_ref.shape
    devices, held, _ = out_ref.shape
    capacity = held - TAIL
    index = received_ref[:, 0, : 2 * capacity]
    half = devices // 2
    lane = lax.broadcasted_iota(jnp.int32, (half, 2 * capacity), 1)
    index = jnp.where(lane < capacity, index[:half], pltpu.roll(index[half:], capacity, 1))
    index_vmem[...] = index.astype(jnp.int32)
    index_copies = []
    for piece in range(INDEX_PIECES):
        span = pl.ds(piece * (half // INDEX_PIECES), half // INDEX_PIECES)
        index_copies.append(pltpu.make_async_copy(index_vmem.at[span], index_ref.at[span], index_sems.at[piece]))
        index_copies[-1].start()
    row = jnp.sum(received_ref[:, 0, 2 * capacity :], axis=0, keepdims=True)
    high, rest = split(row)
    low, _ = split(row - high.astype(jnp.float32) - rest.astype(jnp.float32))
    terms = [high.astype(jnp.float32), rest.astype(jnp.float32), low.astype(jnp.float32)]
    tail = jnp.concatenate(terms + [jnp.zeros((TAIL - 3, features), jnp.float32)], axis=0).astype(jnp.bfloat16)
    for start in range(0, items, 256):
        wide_ref[start : start + 256, :] = table_ref[start : start + 256, :].astype(jnp.float32)
    for at in range(half):
        if at % (half // INDEX_PIECES) == 0:
            index_copies[at // (half // INDEX_PIECES)].wait()
        for device, place in ((at, 0), (half + at, capacity)):
            rows = [wide_ref[pl.ds(index_ref[at, place + slot], 1), :] for slot in range(capacity)]
            out_ref[device, :capacity, :] = jnp.concatenate(rows, axis=0).astype(jnp.bfloat16)
            out_ref[device, capacity:, :] = tail


def fetch_rows(received, item_table, capacity):
    devices = received.shape[0]
    items, features = item_table.shape
    vmem = pl.BlockSpec(memory_space=pltpu.VMEM)
    return pl.pallas_call(
        fetch_kernel,
        out_shape=jax.ShapeDtypeStruct((devices, capacity + TAIL, features), jnp.bfloat16),
        in_specs=[vmem, vmem],
        out_specs=vmem,
        scratch_shapes=[
            pltpu.VMEM((items, features), jnp.float32),
            pltpu.VMEM((devices // 2, 2 * capacity), jnp.int32),
            pltpu.SMEM((devices // 2, 2 * capacity), jnp.int32),
            pltpu.SemaphoreType.DMA((INDEX_PIECES,)),
        ],
        compiler_params=pltpu.CompilerParams(vmem_limit_bytes=FETCH_LIMIT),
        cost_estimate=pl.CostEstimate(flops=0, bytes_accessed=24 * 2**20, transcendentals=0),
    )(received, item_table)


def split(value):
    high = value.astype(jnp.bfloat16)
    low = (value - high.astype(jnp.float32)).astype(jnp.bfloat16)
    return high, low


def solve_kernel(
    total_items,
    slots_hbm,
    arrived_ref,
    weights_ref,
    counts_ref,
    start_ref,
    out_ref,
    wide_ref,
    shared_ref,
    conf_ref,
    system_ref,
    slots_ref,
    slots_sem,
):
    users, links = slots_ref.shape
    devices, held, features = arrived_ref.shape
    slots_copy = pltpu.make_async_copy(slots_hbm, slots_ref, slots_sem)
    slots_copy.start()
    capacity = held - TAIL

    def widen(device, carry):
        start = pl.multiple_of(device * capacity, capacity)
        wide_ref[pl.ds(start, capacity), :] = arrived_ref[device, :capacity, :].astype(jnp.float32)
        tail = arrived_ref[device, capacity:, :].astype(jnp.float32)
        shared_ref[pl.ds(device, 1), :] = jnp.sum(tail, axis=0, keepdims=True)
        return carry

    lax.fori_loop(0, devices, widen, 0, unroll=8)
    diagonal = jnp.where(
        lax.broadcasted_iota(jnp.int32, (features, features), 0)
        == lax.broadcasted_iota(jnp.int32, (features, features), 1),
        0.5 * links,
        0.0,
    )
    shared_ref[...] = shared_ref[...] * (links / total_items) + diagonal
    link_id = lax.broadcasted_iota(jnp.int32, (users, links), 1)
    conf_ref[...] = jnp.where(
        link_id < counts_ref[...], 1.0 + weights_ref[...].astype(jnp.float32) / 8.0, 0.0
    )
    lane = lax.broadcasted_iota(jnp.int32, (1, 2 * users), 1)
    user_lane = jnp.where(lane < users, lane, lane - users)
    ones = jnp.ones((links, 2 * users), jnp.bfloat16)

    def stationary(vector):
        high, low = split(vector)
        half = jnp.where(lane < users, high.astype(jnp.float32), low.astype(jnp.float32)).astype(jnp.bfloat16)
        return jnp.concatenate([half, half], axis=0)

    def both_halves(image):
        return image + pltpu.roll(image, users, 1)

    def form(user, target):
        rows = [wide_ref[pl.ds(slots_ref[user, link], 1), :] for link in range(links)]
        fetched = jnp.concatenate(rows, axis=0)
        scaled = (fetched.T * conf_ref[user : user + 1, :]).astype(jnp.bfloat16)
        both = jnp.dot(
            scaled,
            jnp.concatenate([fetched.astype(jnp.bfloat16), ones], axis=1),
            preferred_element_type=jnp.float32,
        )
        system = jnp.concatenate(split(both[:, :features] + shared_ref[...]), axis=1)
        system_ref[user * features : (user + 1) * features, :] = system
        return jnp.where(user_lane == user, both[:, features:], target)

    def apply_some(user, count, operand, image):
        product = jnp.dot(
            system_ref[user * features : (user + count) * features, :], operand, preferred_element_type=jnp.float32
        )
        for one in range(count):
            piece = product[one * features : (one + 1) * features]
            image = jnp.where(user_lane == user + one, piece, image)
        return image

    def refine(first, last, target, image, estimate):
        residual = target - both_halves(image)
        direction = residual
        norm_now = jnp.sum(residual * residual, axis=0, keepdims=True)
        for iteration in range(CG_STEPS):
            operand = stationary(direction)
            image = jnp.zeros_like(direction)
            for user in range(first, last, TOGETHER):
                image = apply_some(user, TOGETHER, operand, image)
            yield None
            image = both_halves(image)
            curvature = jnp.sum(direction * image, axis=0, keepdims=True)
            step_len = norm_now / (curvature + 1e-06)
            estimate = estimate + step_len * direction
            residual = residual - step_len * image
            norm_next = jnp.sum(residual * residual, axis=0, keepdims=True)
            direction = residual + norm_next / (norm_now + 1e-06) * direction
            norm_now = norm_next
        yield estimate

    start_rows = start_ref[...]
    estimate = jnp.concatenate([start_rows, start_rows], axis=0).T
    operand = stationary(estimate)
    zero = jnp.zeros((features, 2 * users), jnp.float32)
    slots_copy.wait()
    chains, last = [], 0
    for batch in BATCHES:
        first, last = last, last + batch
        target, image = zero, zero
        for user in range(first, last):
            target = form(user, target)
            if (user + 1) % FORMED == 0:
                image = apply_some(user + 1 - FORMED, FORMED, operand, image)
        chains.append(refine(first, last, target, image, estimate if not chains else zero))
    total = zero
    for _ in range(CG_STEPS + 1):
        done = [next(chain) for chain in chains]
    for one in done:
        total = total + one
    out_ref[...] = total.T[:users]


def solve_rows(link_slots, arrived, link_weights, link_counts, user_rows, total_items):
    users, links = link_slots.shape
    features = user_rows.shape[1]
    vmem = pl.BlockSpec(memory_space=pltpu.VMEM)
    return pl.pallas_call(
        functools.partial(solve_kernel, total_items),
        out_shape=jax.ShapeDtypeStruct((users, features), jnp.float32),
        in_specs=[pl.BlockSpec(memory_space=pl.ANY)] + [vmem] * 4,
        out_specs=vmem,
        scratch_shapes=[
            pltpu.VMEM((users * links, features), jnp.float32),
            pltpu.VMEM((features, features), jnp.float32),
            pltpu.VMEM((users, links), jnp.float32),
            pltpu.VMEM((users * features, 2 * features), jnp.bfloat16),
            pltpu.SMEM((users, links), jnp.int32),
            pltpu.SemaphoreType.DMA,
        ],
        compiler_params=pltpu.CompilerParams(vmem_limit_bytes=SOLVE_LIMIT),
        cost_estimate=pl.CostEstimate(flops=2**32, bytes_accessed=24 * 2**20, transcendentals=0),
    )(link_slots, arrived, link_weights, link_counts.reshape(users, 1), user_rows)


def exchange(value):
    return lax.all_to_all(value, AXES, split_axis=0, concat_axis=0, tiled=True)


def per_device(item_table, user_rows, link_rows, link_slots, link_weights, link_counts):
    users, features = user_rows.shape
    links = link_rows.shape[1]
    devices = lax.axis_size("rows") * lax.axis_size("table")
    capacity = users * links // devices
    total_items = item_table.shape[0] * devices
    received = exchange(ask(link_slots, link_rows, item_table, devices))
    arrived = exchange(fetch_rows(received, item_table, capacity))
    return solve_rows(link_slots, arrived, link_weights, link_counts, user_rows, total_items)


def solution(mesh):
    placed = (P(AXES, None),) * 5 + (P(AXES),)
    return jax.shard_map(
        per_device,
        mesh=mesh,
        in_specs=placed,
        out_specs=P(AXES, None),
        check_vma=False,
    )
```

```python
import functools

import jax
import jax.numpy as jnp
from jax import lax
from jax.experimental import pallas as pl
from jax.experimental.pallas import tpu as pltpu
from jax.sharding import PartitionSpec as P

CG_STEPS = 3
BATCHES = (32, 32)
TOGETHER = 8
FORMED = 16
AXES = ("rows", "table")
VMEM_LIMIT = 56 * 2**20
FETCH_LIMIT = 24 * 2**20
SOLVE_LIMIT = 24 * 2**20
NT = (((1,), (1,)), ((), ()))
TN = (((0,), (0,)), ((), ()))
TABLE_STEP = 2048
OUT_STEP = 8
INDEX_PIECES = 4
PLACE_FIRST = 32
TAIL = 8


def ask_kernel(slots_hbm, rows_hbm, table_hbm, out_ref, slots_ref, rows_ref, table_ref, sems):
    half = table_ref.shape[0] // 2
    copies = [
        pltpu.make_async_copy(source, target, sems.at[at])
        for at, (source, target) in enumerate(
            (
                (slots_hbm, slots_ref),
                (rows_hbm, rows_ref),
                (table_hbm.at[pl.ds(0, half)], table_ref.at[pl.ds(0, half)]),
                (table_hbm.at[pl.ds(half, half)], table_ref.at[pl.ds(half, half)]),
            )
        )
    ]
    for copy in copies:
        copy.start()
    users, links = slots_ref.shape
    devices = out_ref.shape[0]
    items, features = table_ref.shape
    capacity = users * links // devices
    owner_id = lax.broadcasted_iota(jnp.int32, (devices, links), 0)
    lane_id = lax.broadcasted_iota(jnp.int32, (2 * capacity, links), 0)
    upper = lane_id < capacity
    slot_id = jnp.where(upper, lane_id, lane_id - capacity)
    copies[0].wait()
    copies[1].wait()

    def place(user, total):
        owners, named = [], []
        for one in (user, user + 1):
            slots = slots_ref[one : one + 1, :]
            rows = rows_ref[one : one + 1, :]
            owner = slots // capacity
            place = slots - owner * capacity
            high = (rows // 128).astype(jnp.float32)
            low = (rows % 128).astype(jnp.float32)
            owners.append(jnp.where(owner_id == owner, 1.0, 0.0).astype(jnp.bfloat16))
            value = jnp.where(upper, high, low)
            named.append(jnp.where(slot_id == place, value, 0.0).astype(jnp.bfloat16))
        return total + lax.dot_general(
            jnp.concatenate(owners, axis=1),
            jnp.concatenate(named, axis=1),
            NT,
            preferred_element_type=jnp.float32,
        )

    def add_items(start, gramian):
        block = table_ref[start : start + TABLE_STEP, :]
        return gramian + lax.dot_general(block, block, TN, preferred_element_type=jnp.float32)

    total = jnp.zeros((devices, 2 * capacity), jnp.float32)
    gramian = jnp.zeros((features, features), jnp.float32)
    early = PLACE_FIRST
    for user in range(0, early, 2):
        total = place(user, total)
    copies[2].wait()
    starts = list(range(0, half, TABLE_STEP))
    for user in range(early, users, 2):
        total = place(user, total)
        if starts and (user - early) % 8 == 0:
            gramian = add_items(starts.pop(0), gramian)
    for start in starts:
        gramian = add_items(start, gramian)
    asked = total * 128.0 + pltpu.roll(total, capacity, 1)
    lane = lax.broadcasted_iota(jnp.int32, asked.shape, 1)
    out_ref[:, 0, : 2 * capacity] = jnp.where(lane < capacity, asked, 0.0)
    copies[3].wait()
    for start in range(half, items, TABLE_STEP):
        gramian = add_items(start, gramian)
    out_ref[:, 0, 2 * capacity :] = gramian


def ask(link_slots, link_rows, item_table, devices):
    users, links = link_slots.shape
    features = item_table.shape[1]
    capacity = users * links // devices
    return pl.pallas_call(
        ask_kernel,
        out_shape=jax.ShapeDtypeStruct((devices, 1, 2 * capacity + features), jnp.float32),
        in_specs=[pl.BlockSpec(memory_space=pl.ANY)] * 3,
        out_specs=pl.BlockSpec(memory_space=pltpu.VMEM),
        scratch_shapes=[
            pltpu.VMEM(link_slots.shape, jnp.int32),
            pltpu.VMEM(link_rows.shape, jnp.int32),
            pltpu.VMEM(item_table.shape, jnp.bfloat16),
            pltpu.SemaphoreType.DMA((4,)),
        ],
        compiler_params=pltpu.CompilerParams(vmem_limit_bytes=VMEM_LIMIT),
        cost_estimate=pl.CostEstimate(flops=2**30, bytes_accessed=2**22, transcendentals=0),
    )(link_slots, link_rows, item_table)


def fetch_kernel(received_ref, table_ref, out_hbm, wide_ref, index_vmem, index_ref, out_ref, index_sems, out_sems):
    items, features = table_ref.shape
    devices, held, _ = out_ref.shape
    capacity = held - TAIL
    index = received_ref[:, 0, : 2 * capacity]
    half = devices // 2
    lane = lax.broadcasted_iota(jnp.int32, (half, 2 * capacity), 1)
    index = jnp.where(lane < capacity, index[:half], pltpu.roll(index[half:], capacity, 1))
    index_vmem[...] = index.astype(jnp.int32)
    index_copies = []
    for piece in range(INDEX_PIECES):
        span = pl.ds(piece * (half // INDEX_PIECES), half // INDEX_PIECES)
        index_copies.append(pltpu.make_async_copy(index_vmem.at[span], index_ref.at[span], index_sems.at[piece]))
        index_copies[-1].start()
    row = jnp.sum(received_ref[:, 0, 2 * capacity :], axis=0, keepdims=True)
    high, rest = split(row)
    low, _ = split(row - high.astype(jnp.float32) - rest.astype(jnp.float32))
    terms = [high.astype(jnp.float32), rest.astype(jnp.float32), low.astype(jnp.float32)]
    tail = jnp.concatenate(terms + [jnp.zeros((TAIL - 3, features), jnp.float32)], axis=0).astype(jnp.bfloat16)
    for start in range(0, items, 256):
        wide_ref[start : start + 256, :] = table_ref[start : start + 256, :].astype(jnp.float32)
    sent = []
    for at in range(half):
        if at % (half // INDEX_PIECES) == 0:
            index_copies[at // (half // INDEX_PIECES)].wait()
        for device, place in ((at, 0), (half + at, capacity)):
            rows = [wide_ref[pl.ds(index_ref[at, place + slot], 1), :] for slot in range(capacity)]
            out_ref[device, :capacity, :] = jnp.concatenate(rows, axis=0).astype(jnp.bfloat16)
            out_ref[device, capacity:, :] = tail
        if (at + 1) % OUT_STEP == 0:
            for end in (at + 1, half + at + 1):
                span = pl.ds(end - OUT_STEP, OUT_STEP)
                sent.append(pltpu.make_async_copy(out_ref.at[span], out_hbm.at[span], out_sems.at[len(sent)]))
                sent[-1].start()
    for copy in sent:
        copy.wait()


def fetch_rows(received, item_table, capacity):
    devices = received.shape[0]
    items, features = item_table.shape
    vmem = pl.BlockSpec(memory_space=pltpu.VMEM)
    return pl.pallas_call(
        fetch_kernel,
        out_shape=jax.ShapeDtypeStruct((devices, capacity + TAIL, features), jnp.bfloat16),
        in_specs=[vmem, vmem],
        out_specs=pl.BlockSpec(memory_space=pl.ANY),
        scratch_shapes=[
            pltpu.VMEM((items, features), jnp.float32),
            pltpu.VMEM((devices // 2, 2 * capacity), jnp.int32),
            pltpu.SMEM((devices // 2, 2 * capacity), jnp.int32),
            pltpu.VMEM((devices, capacity + TAIL, features), jnp.bfloat16),
            pltpu.SemaphoreType.DMA((INDEX_PIECES,)),
            pltpu.SemaphoreType.DMA((devices // OUT_STEP,)),
        ],
        compiler_params=pltpu.CompilerParams(vmem_limit_bytes=FETCH_LIMIT),
        cost_estimate=pl.CostEstimate(flops=0, bytes_accessed=24 * 2**20, transcendentals=0),
    )(received, item_table)


def split(value):
    high = value.astype(jnp.bfloat16)
    low = (value - high.astype(jnp.float32)).astype(jnp.bfloat16)
    return high, low


def solve_kernel(
    total_items,
    slots_hbm,
    arrived_ref,
    weights_ref,
    counts_ref,
    start_ref,
    out_ref,
    wide_ref,
    shared_ref,
    conf_ref,
    system_ref,
    slots_ref,
    slots_sem,
):
    users, links = slots_ref.shape
    devices, held, features = arrived_ref.shape
    slots_copy = pltpu.make_async_copy(slots_hbm, slots_ref, slots_sem)
    slots_copy.start()
    capacity = held - TAIL

    def widen(device, carry):
        start = pl.multiple_of(device * capacity, capacity)
        wide_ref[pl.ds(start, capacity), :] = arrived_ref[device, :capacity, :].astype(jnp.float32)
        tail = arrived_ref[device, capacity:, :].astype(jnp.float32)
        shared_ref[pl.ds(device, 1), :] = jnp.sum(tail, axis=0, keepdims=True)
        return carry

    lax.fori_loop(0, devices, widen, 0, unroll=32)
    diagonal = jnp.where(
        lax.broadcasted_iota(jnp.int32, (features, features), 0)
        == lax.broadcasted_iota(jnp.int32, (features, features), 1),
        0.5 * links,
        0.0,
    )
    shared_ref[...] = shared_ref[...] * (links / total_items) + diagonal
    link_id = lax.broadcasted_iota(jnp.int32, (users, links), 1)
    conf_ref[...] = jnp.where(
        link_id < counts_ref[...], 1.0 + weights_ref[...].astype(jnp.float32) / 8.0, 0.0
    )
    lane = lax.broadcasted_iota(jnp.int32, (1, 2 * users), 1)
    user_lane = jnp.where(lane < users, lane, lane - users)
    ones = jnp.ones((links, 2 * users), jnp.bfloat16)

    def stationary(vector):
        high, low = split(vector)
        half = jnp.where(lane < users, high.astype(jnp.float32), low.astype(jnp.float32)).astype(jnp.bfloat16)
        return jnp.concatenate([half, half], axis=0)

    def both_halves(image):
        return image + pltpu.roll(image, users, 1)

    def form(user, target):
        rows = [wide_ref[pl.ds(slots_ref[user, link], 1), :] for link in range(links)]
        fetched = jnp.concatenate(rows, axis=0)
        scaled = (fetched.T * conf_ref[user : user + 1, :]).astype(jnp.bfloat16)
        both = jnp.dot(
            scaled,
            jnp.concatenate([fetched.astype(jnp.bfloat16), ones], axis=1),
            preferred_element_type=jnp.float32,
        )
        system = jnp.concatenate(split(both[:, :features] + shared_ref[...]), axis=1)
        system_ref[user * features : (user + 1) * features, :] = system
        return jnp.where(user_lane == user, both[:, features:], target)

    def apply_some(user, count, operand, image):
        product = jnp.dot(
            system_ref[user * features : (user + count) * features, :], operand, preferred_element_type=jnp.float32
        )
        for one in range(count):
            piece = product[one * features : (one + 1) * features]
            image = jnp.where(user_lane == user + one, piece, image)
        return image

    def refine(first, last, target, image, estimate):
        residual = target - both_halves(image)
        direction = residual
        norm_now = jnp.sum(residual * residual, axis=0, keepdims=True)
        for iteration in range(CG_STEPS):
            operand = stationary(direction)
            image = jnp.zeros_like(direction)
            for user in range(first, last, TOGETHER):
                image = apply_some(user, TOGETHER, operand, image)
            yield None
            image = both_halves(image)
            curvature = jnp.sum(direction * image, axis=0, keepdims=True)
            step_len = norm_now / (curvature + 1e-06)
            estimate = estimate + step_len * direction
            residual = residual - step_len * image
            norm_next = jnp.sum(residual * residual, axis=0, keepdims=True)
            direction = residual + norm_next / (norm_now + 1e-06) * direction
            norm_now = norm_next
        yield estimate

    start_rows = start_ref[...]
    estimate = jnp.concatenate([start_rows, start_rows], axis=0).T
    operand = stationary(estimate)
    zero = jnp.zeros((features, 2 * users), jnp.float32)
    slots_copy.wait()
    chains, last = [], 0
    for batch in BATCHES:
        first, last = last, last + batch
        target, image = zero, zero
        for user in range(first, last):
            target = form(user, target)
            if (user + 1) % FORMED == 0:
                image = apply_some(user + 1 - FORMED, FORMED, operand, image)
        chains.append(refine(first, last, target, image, estimate if not chains else zero))
    total = zero
    for _ in range(CG_STEPS + 1):
        done = [next(chain) for chain in chains]
    for one in done:
        total = total + one
    out_ref[...] = total.T[:users]


def solve_rows(link_slots, arrived, link_weights, link_counts, user_rows, total_items):
    users, links = link_slots.shape
    features = user_rows.shape[1]
    vmem = pl.BlockSpec(memory_space=pltpu.VMEM)
    return pl.pallas_call(
        functools.partial(solve_kernel, total_items),
        out_shape=jax.ShapeDtypeStruct((users, features), jnp.float32),
        in_specs=[pl.BlockSpec(memory_space=pl.ANY)] + [vmem] * 4,
        out_specs=vmem,
        scratch_shapes=[
            pltpu.VMEM((users * links, features), jnp.float32),
            pltpu.VMEM((features, features), jnp.float32),
            pltpu.VMEM((users, links), jnp.float32),
            pltpu.VMEM((users * features, 2 * features), jnp.bfloat16),
            pltpu.SMEM((users, links), jnp.int32),
            pltpu.SemaphoreType.DMA,
        ],
        compiler_params=pltpu.CompilerParams(vmem_limit_bytes=SOLVE_LIMIT),
        cost_estimate=pl.CostEstimate(flops=2**32, bytes_accessed=24 * 2**20, transcendentals=0),
    )(link_slots, arrived, link_weights, link_counts.reshape(users, 1), user_rows)


def exchange(value):
    return lax.all_to_all(value, AXES, split_axis=0, concat_axis=0, tiled=True)


def per_device(item_table, user_rows, link_rows, link_slots, link_weights, link_counts):
    users, features = user_rows.shape
    links = link_rows.shape[1]
    devices = lax.axis_size("rows") * lax.axis_size("table")
    capacity = users * links // devices
    total_items = item_table.shape[0] * devices
    received = exchange(ask(link_slots, link_rows, item_table, devices))
    arrived = exchange(fetch_rows(received, item_table, capacity))
    return solve_rows(link_slots, arrived, link_weights, link_counts, user_rows, total_items)


def solution(mesh):
    placed = (P(AXES, None),) * 5 + (P(AXES),)
    return jax.shard_map(
        per_device,
        mesh=mesh,
        in_specs=placed,
        out_specs=P(AXES, None),
        check_vma=False,
    )
```
